32 devices in a mesh: dp: 16 (over z, x, core), tensor: 2 (over y).
Axes of the slice: x: 2, y: 2, z: 4, core: 2. Of those that a mesh axis runs over, the one named last changes fastest.
Arguments:
- tokens: bfloat16 [32768, 312], P('dp'), may hold values from -6 to 6
- projection: bfloat16 [3, 312, 312], P(None, None, 'tensor'), may hold values from -0.3125 to 0.3125
- offsets: bfloat16 [2, 312], P(None, 'tensor'), may hold values from -3 to 3
- combiner: bfloat16 [312, 312], P('tensor'), may hold values from -3 to 3
- expansion: bfloat16 [312, 1200], P(None, 'tensor'), may hold values from -0.3125 to 0.3125
- thresholds: bfloat16 [1200], P('tensor'), may hold values from -3 to 3
- contraction: bfloat16 [1200, 312], P('tensor'), may hold values from -0.25 to 0.25
- corrections: bfloat16 [2, 312], replicated, may hold values from -3 to 3
- gains: bfloat16 [2, 312], replicated, may hold values from 0.5 to 1.5
- shifts: bfloat16 [2, 312], replicated, may hold values from -3 to 3
- table_rows: int32 [32768], P('dp'), may hold values from 0 to 168, as said below
- table_columns: int32 [32768], P('dp'), may hold values from 0 to 60, as said below
- table_lengths: int32 [32], P('dp'), may hold values from 256 to 1024
- cotangent: bfloat16 [32768, 312], P('dp'), may hold values from -6 to 6
Outputs:
- layer_output: bfloat16 [32768, 312], P('dp')
- input_gradient: float32 [32768, 312], P('dp')
- projection_gradient: float32 [3, 312, 312], P(None, None, 'tensor')
- offsets_gradient: float32 [2, 312], P(None, 'tensor')
- combiner_gradient: float32 [312, 312], P('tensor')
- expansion_gradient: float32 [312, 1200], P(None, 'tensor')
- thresholds_gradient: float32 [1200], P('tensor')
- contraction_gradient: float32 [1200, 312], P('tensor')
- corrections_gradient: float32 [2, 312], replicated
- gains_gradient: float32 [2, 312], replicated
- shifts_gradient: float32 [2, 312], replicated
The draws below stay inside these ranges and needn't reach their ends.
Inputs may be any that keep to these rules, and one draw needn't show every extreme that they name: `table_rows`: in every table slots 0 to 15 have row 0 and column 0; a table's cells have rows from 1 and columns from 1 upward. `table_columns`: one table is laid out with 60 columns; others with 3 to 60.
All inputs are finite; a program needn't handle non-finite values.
Results may differ from the reference program's by a relative error of at most 0.02.
Values may be sent and summed in bfloat16 or wider, within the bound.
A program may use at most 128 MiB of HBM per device.

```python
import jax
import jax.numpy as jnp
from jax import lax

D = 312
HEADS = 12
HEAD_DIM = 26
FF = 1200
L = 1024
TABLES = 32
TOKENS = 32768
N_TENSOR = 2


def cell_layout(key):
    first_key, second_key, third_key, fourth_key, fifth_key, sixth_key = jax.random.split(key, 6)
    narrow = jax.random.randint(first_key, (TABLES,), 3, 17)
    broad = jax.random.randint(second_key, (TABLES,), 41, 61)
    pick = jax.random.randint(third_key, (TABLES,), 0, 12)
    counts = jnp.where(pick == 0, broad, narrow)
    tokens_cell = jax.random.randint(fourth_key, (TABLES,), 2, 7)
    tall = jax.random.randint(fifth_key, (), 0, TABLES)
    wide = (tall + 1 + jax.random.randint(sixth_key, (), 0, TABLES - 1)) % TABLES
    counts = counts.at[tall].set(3).at[wide].set(60)
    tokens_cell = tokens_cell.at[tall].set(2).at[wide].set(2)
    places = jnp.arange(L, dtype=jnp.int32)
    cells = jnp.maximum(places[None, :] - 16, 0) // tokens_cell[:, None]
    header = places[None, :] < 16
    rows = jnp.where(header, 0, 1 + cells // counts[:, None])
    columns = jnp.where(header, 0, 1 + cells % counts[:, None])
    return (rows.reshape(TOKENS).astype(jnp.int32), columns.reshape(TOKENS).astype(jnp.int32))


def draw_table_rows(key, part):
    rows, columns = cell_layout(key)
    return rows


def draw_table_columns(key, part):
    rows, columns = cell_layout(key)
    return columns


def draw_table_lengths(key, part):
    key = jax.random.fold_in(key, 3)
    first_key, second_key, third_key = jax.random.split(key, 3)
    lengths = jax.random.randint(first_key, (TABLES,), L // 4, L + 1)
    where = jax.random.randint(second_key, (), 0, TABLES)
    other = (where + 1 + jax.random.randint(third_key, (), 0, TABLES - 1)) % TABLES
    return lengths.at[where].set(L).at[other].set(L // 4).astype(jnp.int32)


def levels(rng, shape, shards, smallest, high):
    level, own = 1.0, jax.random.fold_in(rng, 6)
    for dim, parts in shards:
        steps = jnp.exp(jax.random.uniform(jax.random.fold_in(own, dim), (parts,), jnp.float32, smallest / len(shards), high / len(shards)))
        level = level * jnp.repeat(steps, shape[dim] // parts).reshape([-1 if axis == dim else 1 for axis in range(len(shape))])
    return level


def scatter_about(key, shape, deviation, limit, cuts=(), held_as=jnp.bfloat16):
    values = jax.random.normal(key, shape, jnp.float32) * deviation
    if len(cuts) > 0:
        values = levels(key, shape, cuts, -0.22, 0.18) * values
    return jnp.clip(values, min=-limit, max=limit).astype(held_as)


def setup_inputs(seed: int = 0) -> dict:
    streams_of = jax.random.split(jax.random.key(seed), 15)
    return {
        "tokens": scatter_about(streams_of[0], (TOKENS, D), 1.0, 6.0, ((0, 16),)),
        "projection": scatter_about(streams_of[1], (3, D, D), D ** -0.5, 0.3125, ((2, 2),)),
        "offsets": scatter_about(streams_of[2], (2, D), 0.3, 3.0, ((1, 2),)),
        "combiner": scatter_about(streams_of[3], (D, D), (max(2, D // 64)) ** -0.5, 3.0, ((0, 2),)),
        "expansion": scatter_about(streams_of[4], (D, FF), D ** -0.5, 0.3125, ((1, 2),)),
        "thresholds": scatter_about(streams_of[5], (FF,), 0.5, 3.0, ((0, 2),)),
        "contraction": scatter_about(streams_of[6], (FF, D), (FF // 2) ** -0.5, 0.25, ((0, 2),)),
        "corrections": scatter_about(streams_of[7], (2, D), 0.3, 3.0),
        "gains": jnp.clip(1.0 + 0.1 * jax.random.normal(streams_of[8], (2, D), jnp.float32), 0.5, 1.5).astype(jnp.bfloat16),
        "shifts": scatter_about(streams_of[9], (2, D), 0.3, 3.0),
        "table_rows": draw_table_rows(jax.random.fold_in(streams_of[14], 71), 0),
        "table_columns": draw_table_columns(jax.random.fold_in(streams_of[14], 71), 0),
        "table_lengths": draw_table_lengths(jax.random.fold_in(streams_of[14], 71), 0),
        "cotangent": scatter_about(streams_of[13], (TOKENS, D), 1.0, 6.0, ((0, 16),)),
    }


EPS = 1e-05
MASKED = -1e+30
HIGHEST = lax.Precision.HIGHEST

@jax.custom_vjp
def low(v):
    return lax.optimization_barrier(v.astype(jnp.bfloat16)).astype(jnp.float32)

@jax.custom_vjp
def low_back(v):
    return v

def low_keep(v):
    return (low(v), None)

def low_pass(kept, grad):
    return (grad,)

def back_keep(v):
    return (v, None)

def back_low(kept, grad):
    return (low(grad),)
low.defvjp(low_keep, low_pass)
low_back.defvjp(back_keep, back_low)

def rounded(value):
    return low_back(low(value))

def layer_norm(resid, gain, shift):
    center = resid - lax.optimization_barrier(jnp.mean(resid, -1, keepdims=True))
    spread = lax.optimization_barrier(jnp.mean(center * center, -1, keepdims=True))
    return center * lax.rsqrt(spread + EPS) * gain + shift

def attend_table(pieces):
    query, keys, values, rows, columns, length = pieces
    scores = jnp.einsum('qhe,khe->hqk', query, keys, precision=HIGHEST) * HEAD_DIM ** (-0.5)
    scores = low_back(scores)
    places = jnp.arange(L)
    seen = (rows[:, None] == rows[None, :]) | (columns[:, None] == columns[None, :])
    seen = seen | (rows[None, :] == 0) | (rows[:, None] == 0)
    seen = seen & (places[None, :] < length)
    scores = jnp.where(seen[None], scores, MASKED)
    expo = jnp.exp(scores - lax.optimization_barrier(jnp.max(scores, -1, keepdims=True)))
    probs = low(expo / lax.optimization_barrier(jnp.sum(expo, -1, keepdims=True)))
    return jnp.einsum('hqk,khe->qhe', probs, values, precision=HIGHEST)

def reference(tokens, projection, offsets, combiner, expansion, thresholds, contraction, corrections, gains, shifts, table_rows, table_columns, table_lengths, cotangent):
    floats = tuple((a.astype(jnp.float32) for a in (tokens, projection, offsets, combiner, expansion, thresholds, contraction, corrections, gains, shifts)))
    width = D // N_TENSOR
    span = FF // N_TENSOR
    shaped = (TABLES, L, HEADS, HEAD_DIM)

    def forward(inputs, w_qkv, biases, w_out, w_up, b_up, w_down, b_res, gain_pair, shift_pair):
        inputs_low = low(inputs)
        projected = jnp.einsum('td,cde->cte', inputs_low, w_qkv, precision=HIGHEST)
        query = rounded(projected[0] + biases[0])
        keys = rounded(projected[1])
        values = rounded(projected[2] + biases[1])
        context = lax.map(jax.checkpoint(attend_table), (query.reshape(shaped), keys.reshape(shaped), values.reshape(shaped), table_rows.reshape(TABLES, L), table_columns.reshape(TABLES, L), table_lengths))
        context = rounded(context.reshape(TOKENS, D))
        attended = jnp.zeros((TOKENS, D), jnp.float32)
        for shard in range(N_TENSOR):
            attended = attended + low(jnp.dot(context[:, shard * width:(shard + 1) * width], w_out[shard * width:(shard + 1) * width], precision=HIGHEST))
        first = layer_norm(inputs + low_back(attended) + b_res[0], gain_pair[0], shift_pair[0])
        first_low = low(first)
        pre = low_back(jnp.dot(first_low, w_up, precision=HIGHEST) + b_up)
        act = low(jax.nn.gelu(pre, approximate=False))
        down = jnp.zeros((TOKENS, D), jnp.float32)
        for shard in range(N_TENSOR):
            down = down + low(jnp.dot(act[:, shard * span:(shard + 1) * span], w_down[shard * span:(shard + 1) * span], precision=HIGHEST))
        return layer_norm(first + low_back(down) + b_res[1], gain_pair[1], shift_pair[1])
    result, pullback = jax.vjp(forward, *floats)
    grads = pullback(cotangent.astype(jnp.float32))
    return (result.astype(jnp.bfloat16), grads[0], grads[1], grads[2], grads[3], grads[4], grads[5], grads[6], grads[7], grads[8], grads[9])
```

```python
import functools
import jax
import jax.numpy as jnp
from jax import lax
from jax.experimental import pallas as pl
from jax.experimental.pallas import tpu as pltpu
from jax.sharding import PartitionSpec as P

HEAD_DIM = 26
PAD = 32
EPS = 1e-05
MASKED = -1e30
SCALE = HEAD_DIM ** -0.5
LOG2E = 1.4426950408889634
BF = jnp.bfloat16
F32 = jnp.float32
NN = (((1,), (0,)), ((), ()))
NT = (((1,), (1,)), ((), ()))
TN = (((0,), (0,)), ((), ()))


def mm(a, b, dims=NN):
    return lax.dot_general(a, b, dims, preferred_element_type=F32)


def phi_pair(x):
    z = jnp.abs(x)
    t = 1.0 / (1.0 + (0.3275911 * 0.5 ** 0.5) * z)
    e = jnp.exp2(x * x * (-0.5 * LOG2E))
    poly = ((((1.061405429 * t - 1.453152027) * t + 1.421413741) * t - 0.284496736) * t + 0.254829592) * t
    tail = 0.5 * poly * e
    return jnp.where(x < 0, tail, 1.0 - tail), e * 0.3989422804014327


def body(
    tokens, cot, proj, offs, comb, up_in, thr_in, down_in, corr, gains, shifts, rows, cols, length,
    out_ref, dx_ref, dwt_ref, dcp_ref, dup_ref, ddown_ref, dsmall_ref,
    wt, cp, up, down, qkv, bias, probs, ctx32, ctx, inv, dctx, dxt, act, dgel, dpre, first_low, d_down, d_att, tok_aug, off_buf, rk_buf, ck_buf, k_buf, sem,
):
    T, D = tokens.shape
    shards = proj.shape[0]
    part = proj.shape[3]
    hs = part // HEAD_DIM
    heads = shards * hs
    width = hs * PAD
    hid = up_in.shape[2]
    hstride = up.shape[1] // shards
    BQ = 256

    r = lax.broadcasted_iota(jnp.int32, (width, part), 0)
    c = lax.broadcasted_iota(jnp.int32, (width, part), 1)
    inside = (r & (PAD - 1)) < HEAD_DIM
    sel = jnp.where(inside & (c == r - (PAD - HEAD_DIM) * (r >> 5)), 1.0, 0.0).astype(BF)
    up[...] = jnp.zeros_like(up)
    down[...] = jnp.zeros_like(down)
    for s in range(shards):
        for p in range(3):
            wt[pl.ds(p * heads * PAD + s * width, width), :] = mm(sel, proj[s, p], NT).astype(BF)
        cp[pl.ds(s * width, width), :] = mm(sel, comb[s]).astype(BF)
        up[:, s * hstride : s * hstride + hid] = up_in[s]
        down[s * hstride : s * hstride + hid, :] = down_in[s]
    tok_aug[...] = jnp.zeros_like(tok_aug)
    first_low[...] = jnp.zeros_like(first_low)
    tok_aug[:, 0:D] = tokens[...]
    ones = jnp.where(lax.broadcasted_iota(jnp.int32, (T, 128), 1) == D - 256, 1.0, 0.0).astype(BF)
    tok_aug[:, 256:384] = tok_aug[:, 256:384] + ones
    first_low[:, 256:384] = ones

    rr = lax.broadcasted_iota(jnp.int32, (width, 1), 0) & (PAD - 1)
    extra = jnp.where((rr == HEAD_DIM) | (rr == HEAD_DIM + 1), 1.0, 0.0)
    for s in range(shards):
        off = mm(sel, offs[s], NT)
        off_buf[s] = jnp.concatenate([off[:, 0:1], jnp.zeros((width, 1), F32), off[:, 1:2] + extra, jnp.zeros((width, 125), F32)], 1)

    def project(b, carry):
        t = pl.ds(pl.multiple_of(b * 256, 256), 256)
        for s in range(shards):
            for p in range(3):
                x = mm(wt[p * heads * PAD + s * width : p * heads * PAD + (s + 1) * width, :], tokens[t, :], NT)
                x = x + off_buf[s, :, p : p + 1]
                x = (x * (SCALE * LOG2E) if p == 0 else x).astype(BF)
                for h in range(hs):
                    qkv[p, s * hs + h, :, t] = x[h * PAD : (h + 1) * PAD, :]
        return carry

    lax.fori_loop(0, T // 256, project, 0)

    live = lax.broadcasted_iota(jnp.int32, (T, 128), 0) < length[...]
    rk_buf[...] = jnp.where(live, jnp.broadcast_to(rows[...].astype(F32), (128, T)).T, jnp.nan)
    ck_buf[...] = jnp.broadcast_to(cols[...].astype(F32), (128, T)).T

    def visible(j, carry):
        q = pl.ds(pl.multiple_of(j * 128, 128), 128)
        rq = rows[:, q].astype(F32)
        cq = cols[:, q].astype(F32)
        rk = rk_buf[...]
        gap = rk * (rk - rq) * rq * (ck_buf[...] - cq)
        bias[:, q] = jnp.where(gap == 0.0, 0.0, MASKED)
        return carry

    lax.fori_loop(0, T // 128, visible, 0)

    n, KC = T // BQ, 128

    def weigh(h):
        o = mm(qkv[2, h], probs[h])
        i = 1.0 / o[HEAD_DIM : HEAD_DIM + 1, :]
        inv[h] = i
        o = o * i
        ctx32[h] = o
        ctx[pl.ds(pl.multiple_of(h * PAD, PAD), PAD), :] = o.astype(BF)

    def forward_head(h, carry):
        peaks = [None] * n
        kept = {}
        k_buf[...] = qkv[1, h].T

        def score(j, c):
            q, r = slice(j * BQ, (j + 1) * BQ), slice(c * KC, (c + 1) * KC)
            s = mm(k_buf[r, :], qkv[0, h, :, q]) + bias[r, q]
            kept[j, c] = s
            m = jnp.max(s.reshape(KC // 8, 8, BQ), 0)
            peaks[j] = m if c == 0 else jnp.maximum(peaks[j], m)

        def expo(j, c):
            q, r = slice(j * BQ, (j + 1) * BQ), slice(c * KC, (c + 1) * KC)
            if c == 0:
                peaks[j] = jnp.max(peaks[j], 0, keepdims=True)
            probs[h, r, q] = jnp.exp2(kept.pop((j, c)) - peaks[j]).astype(BF)

        for j in range(n + 1):
            for c in range(T // KC):
                if j < n:
                    score(j, c)
                if j > 0:
                    expo(j - 1, c)
        weigh(h)
        return carry

    lax.fori_loop(0, heads, forward_head, 0)

    g0, g1 = gains[0:1, :].astype(F32), gains[1:2, :].astype(F32)
    b0, b1 = shifts[0:1, :].astype(F32), shifts[1:2, :].astype(F32)
    c0, c1 = corr[0:1, :].astype(F32), corr[1:2, :].astype(F32)
    thr = thr_in[...].astype(F32)
    dsmall_ref[...] = jnp.zeros_like(dsmall_ref)

    def norm(x):
        x = x - jnp.mean(x, -1, keepdims=True)
        rs = lax.rsqrt(jnp.mean(x * x, -1, keepdims=True) + EPS)
        return x * rs, rs

    def norm_back(dy, xhat, rs, g):
        d = dy * g
        return rs * (d - jnp.mean(d, -1, keepdims=True) - xhat * jnp.mean(d * xhat, -1, keepdims=True))

    def acc(i, v):
        dsmall_ref[i : i + 1, 0:D] += jnp.sum(v, 0, keepdims=True)

    BT = 256

    def middle(b, carry):
        t = pl.ds(pl.multiple_of(b * BT, BT), BT)
        att = mm(ctx[:, t], cp[...], TN)
        x1, rs1 = norm(tokens[t, :].astype(F32) + att + c0)
        first = x1 * g0 + b0
        low = first.astype(BF)
        first_low[t, 0:256] = low[:, 0:256]
        first_low[t, 256:D] = low[:, 256:D]
        ff = up.shape[1]
        dn = jnp.zeros((BT, D), F32)
        for j in range(ff // 256):
            u = slice(j * 256, (j + 1) * 256)
            pre = mm(low, up[:, u]) + thr[:, u]
            cdf, pdf = phi_pair(pre)
            a = (pre * cdf).astype(BF)
            act[t, u] = a
            dgel[:, u] = (cdf + pre * pdf).astype(BF)
            dn = dn + mm(a, down[u, :])
        x2, rs2 = norm(first + dn + c1)
        out_ref[t, :] = (x2 * g1 + b1).astype(BF)
        dy = cot[t, :].astype(F32)
        acc(0, dy * x2)
        acc(1, dy)
        dr2 = norm_back(dy, x2, rs2, g1)
        acc(2, dr2)
        dd = dr2.astype(BF)
        d_down[t, :] = dd
        df = dr2
        for j in range(ff // 256):
            u = slice(j * 256, (j + 1) * 256)
            dp = (mm(dd, down[u, :], NT) * dgel[:, u].astype(F32)).astype(BF)
            dpre[t, u] = dp
            df = df + mm(dp, up[:, u], NT)
        acc(3, df * x1)
        acc(4, df)
        dr1 = norm_back(df, x1, rs1, g0)
        acc(5, dr1)
        bias[t, 0:D] = dr1
        da = dr1.astype(BF)
        d_att[t, :] = da
        dctx[:, t] = mm(cp[...], da, NT).astype(BF)
        return carry

    lax.fori_loop(0, T // BT, middle, 0)

    def feed_grads(j, carry):
        u = pl.ds(pl.multiple_of(j * 256, 256), 256)
        ddown_ref[:, u] = mm(d_down[...], act[:, u], TN).astype(BF)
        dup_ref[:, u] = mm(first_low[:, 0 : dup_ref.shape[0]], dpre[:, u], TN).astype(BF)
        return carry

    lax.fori_loop(0, up.shape[1] // 256, feed_grads, 0)
    dcp_ref[...] = mm(ctx[...], d_att[...])

    def backward_head(h, carry):
        rowi = lax.broadcasted_iota(jnp.int32, (PAD, T), 0)
        hp = pl.ds(pl.multiple_of(h * PAD, PAD), PAD)
        i = inv[h]
        do = dctx[hp, :].astype(F32)
        nd = jnp.sum(do * ctx32[h], 0, keepdims=True) * (-i)
        hi = nd.astype(BF).astype(F32)
        da = jnp.where(rowi == HEAD_DIM, hi, jnp.where(rowi == HEAD_DIM + 1, nd - hi, do * i)).astype(BF)
        kt = qkv[1, h]
        vt = qkv[2, h]
        qt = qkv[0, h]
        v = vt.T
        hp2 = pl.ds(pl.multiple_of((2 * heads + h) * PAD, PAD), PAD)
        hp1 = pl.ds(pl.multiple_of((heads + h) * PAD, PAD), PAD)
        dq = jnp.zeros((PAD, T), F32)
        for j in range(T // BQ):
            r = slice(j * BQ, (j + 1) * BQ)
            pk = probs[h, r, :]
            dxt[hp2, r] = mm(da, pk, NT).astype(BF)
            ds = (pk.astype(F32) * mm(v[r], da)).astype(BF)
            dxt[hp1, r] = (mm(qt, ds, NT) * (1.0 / LOG2E)).astype(BF)
            dq = dq + mm(kt[:, r], ds)
        dxt[hp, :] = (dq * SCALE).astype(BF)
        return carry

    lax.fori_loop(0, heads, backward_head, 0)

    def weight_grads(p, carry):
        w = pl.ds(pl.multiple_of(p * heads * PAD, PAD), heads * PAD)
        dwt_ref[w, :] = mm(dxt[w, :], tok_aug[...])
        return carry

    lax.fori_loop(0, 3, weight_grads, 0)

    def input_grads(b, carry):
        t = pl.ds(pl.multiple_of(b * BT, BT), BT)
        bias[t, 0:D] = bias[t, 0:D] + mm(dxt[:, t], wt[...], TN)
        return carry

    lax.fori_loop(0, T // BT, input_grads, 0)
    put = pltpu.make_async_copy(bias.at[:, 0:384], dx_ref, sem)
    put.start()
    put.wait()


def compute(tokens, cot, proj, offs, comb, up, thr, down, corr, gains, shifts, rows, cols, length):
    T, D = tokens.shape
    shards, hs = proj.shape[0], proj.shape[3] // HEAD_DIM
    heads = shards * hs
    W = heads * PAD
    FFP = thr.shape[1]
    outs = (
        jax.ShapeDtypeStruct((T, D), BF),
        jax.ShapeDtypeStruct((T, 384), F32),
        jax.ShapeDtypeStruct((3 * W, 384), F32),
        jax.ShapeDtypeStruct((W, D), F32),
        jax.ShapeDtypeStruct((320, FFP), BF),
        jax.ShapeDtypeStruct((D, FFP), BF),
        jax.ShapeDtypeStruct((8, 384), F32),
    )
    ins = (tokens, cot, proj, offs, comb, up, thr, down, corr, gains, shifts, rows, cols, length)
    V = pltpu.VMEM
    scratch = [
        V((3 * W, D), BF), V((W, D), BF), V((D, FFP), BF), V((FFP, D), BF),
        V((3, heads, PAD, T), BF), V((T, T), F32), V((heads, T, T), BF),
        V((heads, PAD, T), F32), V((W, T), BF), V((heads, 1, T), F32), V((W, T), BF), V((3 * W, T), BF),
        V((T, FFP), BF), V((256, FFP), BF), V((T, FFP), BF), V((T, 384), BF), V((T, D), BF), V((T, D), BF), V((T, 384), BF), V((shards, hs * PAD, 128), F32), V((T, 128), F32), V((T, 128), F32), V((T, PAD), BF), pltpu.SemaphoreType.DMA(()),
    ]
    vm = pl.BlockSpec(memory_space=pltpu.VMEM)
    return pl.pallas_call(
        body, out_shape=outs, in_specs=[vm] * len(ins), out_specs=(vm, pl.BlockSpec(memory_space=pl.ANY)) + (vm,) * (len(outs) - 2), scratch_shapes=scratch,
        compiler_params=pltpu.CompilerParams(vmem_limit_bytes=63 * 2 ** 20),
    )(*ins)


def shards(tokens, projection, offsets, combiner, expansion, thresholds, contraction, corrections, gains, shifts, table_rows, table_columns, table_lengths, cotangent):
    two = table_lengths.shape[0]
    T, D = tokens.shape[0] // two, tokens.shape[1]
    part, hid = projection.shape[2], thresholds.shape[0]
    hstride = -(-hid // 128) * 128
    me = lax.axis_index("tensor")
    swap = [(0, 1), (1, 0)]

    def other(x):
        return lax.ppermute(x, "tensor", swap)

    def mine(x):
        return lax.dynamic_index_in_dim(x.reshape((two, T) + x.shape[1:]), me, 0, keepdims=False)

    def pair(x):
        return jnp.stack((x, other(x)))

    offs = jnp.pad(pair(offsets), ((0, 0), (0, 6), (0, 0)))
    thr = jnp.pad(pair(thresholds), ((0, 0), (0, hstride - hid))).reshape(1, two * hstride)
    length = lax.dynamic_slice_in_dim(table_lengths, me, 1).reshape(1, 1)
    out, dx, dwt, dcp, dup, ddown, small = compute(
        mine(tokens), mine(cotangent), pair(projection), offs, pair(combiner), pair(expansion), thr, pair(contraction),
        corrections, gains, shifts, mine(table_rows).reshape(1, T), mine(table_columns).reshape(1, T), length,
    )

    def whole(x):
        y = other(x)
        return jnp.where(me == 0, jnp.concatenate((x, y)), jnp.concatenate((y, x)))

    def reduced(x):
        return lax.psum(x[0].astype(F32) + other(x[1].astype(BF)).astype(F32), "dp")

    hs = part // HEAD_DIM
    dwt = dwt.reshape(3, two, hs, PAD, 384)[:, :, :, :HEAD_DIM, : D + 1].transpose(1, 0, 2, 3, 4).reshape(two, 3, part, D + 1)
    dwt = reduced(dwt)
    dcp = reduced(dcp.reshape(two, hs, PAD, D)[:, :, :HEAD_DIM].reshape(two, part, D))
    dup = reduced(dup.reshape(320, two, hstride)[: D + 1, :, :hid].transpose(1, 0, 2))
    ddown = reduced(ddown.reshape(D, two, hstride)[:, :, :hid].transpose(1, 0, 2))
    small = lax.psum(small, ("dp", "tensor"))[:, :D]
    return (
        whole(out),
        whole(dx[:, :D].astype(BF)).astype(F32),
        dwt[:, :, :D].transpose(0, 2, 1),
        jnp.stack((dwt[0, :, D], dwt[2, :, D])),
        dcp,
        dup[:D],
        dup[D],
        ddown.T,
        jnp.stack((small[5], small[2])),
        jnp.stack((small[3], small[0])),
        jnp.stack((small[4], small[1])),
    )


def solution(mesh):
    return jax.shard_map(
        shards,
        mesh=mesh,
        in_specs=(
            P("dp", None), P(None, None, "tensor"), P(None, "tensor"), P("tensor", None), P(None, "tensor"), P("tensor"),
            P("tensor", None), P(), P(), P(), P("dp"), P("dp"), P("dp"), P("dp", None),
        ),
        out_specs=(
            P("dp", None), P("dp", None), P(None, None, "tensor"), P(None, "tensor"), P("tensor", None), P(None, "tensor"),
            P("tensor"), P("tensor", None), P(), P(), P(),
        ),
        check_vma=False,
    )
```

```python
import functools

import jax
import jax.numpy as jnp
from jax import lax
from jax.experimental import pallas as pl
from jax.experimental.pallas import tpu as pltpu
from jax.sharding import PartitionSpec as P

HEAD_DIM = 26
PAD = 32
TRIPLE = 3 * PAD
EPS = 1e-05
MASKED = -1e30
SCALE = HEAD_DIM ** -0.5
LOG2E = 1.4426950408889634
BF = jnp.bfloat16
F32 = jnp.float32
NN = (((1,), (0,)), ((), ()))
NT = (((1,), (1,)), ((), ()))
TN = (((0,), (0,)), ((), ()))
BT = 256
MESH = pl.DeviceIdType.MESH


def mm(a, b, dims=NN):
    return lax.dot_general(a, b, dims, preferred_element_type=F32)


def up_to(x, m):
    return -(-x // m) * m


def wide(x):
    return jnp.concatenate([x, x], 1)


def phi_pair(x):
    z = jnp.abs(x)
    t = 1.0 / (1.0 + (0.3275911 * 0.5 ** 0.5) * z)
    e = jnp.exp2(x * x * (-0.5 * LOG2E))
    poly = ((((0.5307027145 * t - 0.7265760135) * t + 0.7107068705) * t - 0.142248368) * t + 0.127414796) * t
    tail = poly * e
    return jnp.where(x < 0, tail, 1.0 - tail), e * 0.3989422804014327


def selector(hs):
    r = lax.broadcasted_iota(jnp.int32, (hs * PAD, hs * HEAD_DIM), 0)
    c = lax.broadcasted_iota(jnp.int32, (hs * PAD, hs * HEAD_DIM), 1)
    inside = (r & (PAD - 1)) < HEAD_DIM
    return jnp.where(inside & (c == r - (PAD - HEAD_DIM) * (r >> 5)), 1.0, 0.0).astype(BF)


INPUTS = (
    "tok_in", "cot_in", "proj_in", "comb_in", "up_in", "down_in", "thr_in", "offs_in", "corr_in", "gain_in", "shift_in", "rows_in", "cols_in", "len_in",
)


class Plan:
    def __init__(self, n, hs):
        feed, out = 5 * 160, 5 * (hs * PAD // 4)
        self.parts = PARTS
        self.down, self.up, self.comb, self.small = (0, 0), (1, 0), (1, feed), (1, feed + out)
        self.used = [feed, feed + out + 48] + [5 * (hp * TRIPLE // 4) for hp in self.parts]
        self.first_part = 2
        chain, left = [], n
        while left > 1:
            chain.append(min(4, left))
            left //= chain[-1]
        self.levels = [([n], False) if flat and n <= 8 else (chain, True) for flat in FLAT]
        self.rows = []
        for x, (sizes, swap) in zip(self.used, self.levels):
            cut = 1
            for z in sizes[:-1] if swap else sizes:
                cut *= z
            self.rows.append(up_to(x, 16 * cut))
        self.schedule = SCHEDULE
        self.after = AFTER

    def blocks(self, g):
        sizes, swap = self.levels[g]
        out = [self.rows[g]]
        for j, z in enumerate(sizes):
            out.append(out[-1] if swap and j == len(sizes) - 1 else out[-1] // z)
        return out


PARTS = (4, 2)
FLAT = (False, False, False, True)
SCHEDULE = {0: [(0, 2)], 1: [(1, 2)], 3: [(0, 3)], 5: [(0, 4), (1, 3)], 7: ["part0", (2, 1), (0, 5), (1, 4)], 8: [(2, 2)], 9: [(0, 6), (1, 5)], 10: [(2, 3), (0, 7)], 11: [(1, 6), (2, 4)]}
AFTER = [(3, 1), "w", 0, (3, 2), "send", 1, (1, 7), (2, 5), 2, (3, 3), 3, (2, 6), (3, 4), (2, 7), (3, 5), (3, 6)]


def main_kernel(n, hs, plan, names, *refs):
    r = dict(zip(names, refs))
    tok_in, cot_in, proj_in, comb_in, up_in, down_in, thr_in, offs_in, corr_in, gain_in, shift_in, rows_in, cols_in, len_in = (r[k] for k in INPUTS)
    lo_out, dxo_out, dxp_out = r["lo_out"], r["dxo_out"], r["dxp_out"]
    tok, cot, first_low, d_down, d_att = (r[k] for k in ("tok", "cot", "first_low", "d_down", "d_att"))
    raw_proj, raw_comb, raw_up, raw_down = (r[k] for k in ("raw_proj", "raw_comb", "raw_up", "raw_down"))
    raw_thr, raw_offs, raw_corr, raw_gain, raw_shift = (r[k] for k in ("raw_thr", "raw_offs", "raw_corr", "raw_gain", "raw_shift"))
    wt, cp, cpt, upt, downn = (r[k] for k in ("wt", "cp", "cpt", "upt", "downn"))
    qkv, bias, probs, ctx32, ctx, inv, dctx, dxt, dpre = (
        r[k] for k in ("qkv", "bias", "probs", "ctx32", "ctx", "inv", "dctx", "dxt", "dpre")
    )
    vbuf, thr_buf, off_buf, acc, k_buf = (r[k] for k in ("vbuf", "thr_buf", "off_buf", "acc", "k_buf"))
    rows, cols, lsem, wsend, wrecv, gsend, grecv, gloc, osend, orecv, xsend, xrecv = (
        r[k] for k in ("rows", "cols", "lsem", "wsend", "wrecv", "gsend", "grecv", "gloc", "osend", "orecv", "xsend", "xrecv")
    )
    act = dxt
    D, T = tok.shape
    heads = 2 * hs
    part = hs * HEAD_DIM
    width = hs * PAD
    srows = hs * TRIPLE
    hid = up_in.shape[1]
    hst = upt.shape[0] // 2

    me, dp = lax.axis_index("tensor"), lax.axis_index("dp")
    core, chip = lax.rem(dp, 2), lax.div(dp, 2)
    peer = {"tensor": 1 - me}
    sib = {"dp": dp + 1 - 2 * core}

    def chip_at(k):
        return lax.rem(chip + k, n)

    def on_chip(k):
        return {"dp": chip_at(k) * 2 + core}

    def remote(src, dst, ssem, rsem, dev):
        return pltpu.make_async_remote_copy(src_ref=src, dst_ref=dst, send_sem=ssem, recv_sem=rsem, device_id=dev, device_id_type=MESH)

    mine = pl.ds(pl.multiple_of(me * T, T), T)
    mine8 = pl.ds(pl.multiple_of(me * (T // 128), T // 128), T // 128)
    loads = {}
    for i, (k, a, b) in enumerate((
        ("proj", proj_in, raw_proj.at[0]), ("offs", offs_in, raw_offs.at[0]), ("tok", tok_in.at[:, mine], tok), ("rows", rows_in.at[mine8, :], rows),
        ("cols", cols_in.at[mine8, :], cols), ("comb", comb_in, raw_comb.at[0]), ("up", up_in, raw_up.at[0]), ("down", down_in, raw_down.at[0]),
        ("thr", thr_in, raw_thr.at[0]), ("corr", corr_in, raw_corr), ("gain", gain_in, raw_gain), ("shift", shift_in, raw_shift), ("cot", cot_in.at[:, mine], cot),
    )):
        loads[k] = pltpu.make_async_copy(a, b, lsem.at[i])
        loads[k].start()

    barrier = pltpu.get_barrier_semaphore()
    pl.semaphore_signal(barrier, inc=1, device_id=peer, device_id_type=MESH)
    pl.semaphore_signal(barrier, inc=1, device_id=sib, device_id_type=MESH)
    for k in range(1, n):
        pl.semaphore_signal(barrier, inc=1, device_id=on_chip(k), device_id_type=MESH)

    sel = selector(hs)
    lane = lax.broadcasted_iota(jnp.int32, (PAD, 128), 1)
    sub = lax.broadcasted_iota(jnp.int32, (PAD, 128), 0)
    extra = jnp.where((sub == HEAD_DIM) | (sub == HEAD_DIM + 1), 1.0, 0.0)

    def head_weights(s):
        off = mm(sel, raw_offs[s], NT)
        for p in range(3):
            x = mm(sel, raw_proj[s, p]).astype(BF)
            for h in range(hs):
                a = s * srows + h * TRIPLE + p * PAD
                wt[a : a + PAD, :] = x[h * PAD : (h + 1) * PAD, :]
                if p != 1:
                    col = jnp.broadcast_to(off[h * PAD : (h + 1) * PAD, p // 2 : p // 2 + 1], (PAD, 128))
                    off_buf[a : a + PAD, :] = col + extra if p == 2 else col

    def project(s):
        def block(b, carry):
            t = pl.ds(pl.multiple_of(b * BT, BT), BT)
            x = mm(wt[s * srows : (s + 1) * srows, :], tok[:, t])
            for h in range(hs):
                for p in range(3):
                    a = s * srows + h * TRIPLE + p * PAD
                    y = x[h * TRIPLE + p * PAD : h * TRIPLE + (p + 1) * PAD, :]
                    if p != 1:
                        y = y + wide(off_buf[a : a + PAD, :])
                    if p == 0:
                        y = y * (SCALE * LOG2E)
                    qkv[a : a + PAD, t] = y.astype(BF)
            return carry

        lax.fori_loop(0, T // BT, block, 0)

    loads["proj"].wait()
    loads["offs"].wait()
    head_weights(0)
    loads["tok"].wait()
    project(0)

    pl.semaphore_wait(barrier, n + 1)
    fetched = ((proj_in, raw_proj, 0), (comb_in, raw_comb, 1), (up_in, raw_up, 1), (down_in, raw_down, 1))

    def fetch(i):
        a, b, _ = fetched[i]
        return remote(a, b.at[1], wsend.at[i, 0], wrecv.at[i], peer)

    def hand_on(i):
        b = fetched[i][1]
        return remote(b.at[1], b.at[1], wsend.at[i, 1], wrecv.at[i], sib)

    def only(c, todo, what):
        @pl.when(core == c)
        def _():
            for i in todo:
                what(i)

    def pass_on(i):
        fetch(i).wait()
        hand_on(i).start()

    bias_sends = [
        remote(thr_in, raw_thr.at[1], wsend.at[4, 0], wrecv.at[4], peer),
        remote(offs_in, raw_offs.at[1], wsend.at[5, 0], wrecv.at[5], peer),
    ]
    for cpy in bias_sends:
        cpy.start()
    only(0, (0,), lambda i: fetch(i).start())

    loads["rows"].wait()
    loads["cols"].wait()
    length = jnp.where(me == 0, len_in[0], len_in[1])
    for j in range(T // 128):
        q = slice(j * 128, (j + 1) * 128)
        live = lax.broadcasted_iota(jnp.int32, (128, 128), 0) + j * 128 < length
        thr_buf[q, :] = jnp.where(live, jnp.broadcast_to(rows[j : j + 1, :].astype(F32), (128, 128)).T, jnp.nan)
        vbuf[q, :] = jnp.broadcast_to(cols[j : j + 1, :].astype(F32), (128, 128)).T

    def visible(j, carry):
        q = pl.ds(pl.multiple_of(j * 128, 128), 128)
        rq = rows[pl.ds(j, 1), :].astype(F32)
        cq = cols[pl.ds(j, 1), :].astype(F32)
        rk = thr_buf[0:T, :]
        gap = rk * (rk - rq) * rq * (vbuf[0:T, :] - cq)
        bias[:, q] = jnp.where(gap == 0.0, 0.0, MASKED)
        return carry

    lax.fori_loop(0, T // 128, visible, 0)

    nq, KC = T // BT, 128

    def forward_head(h, carry):
        hq = pl.ds(pl.multiple_of(h * TRIPLE, PAD), PAD)
        hk = pl.ds(pl.multiple_of(h * TRIPLE + PAD, PAD), PAD)
        hv = pl.ds(pl.multiple_of(h * TRIPLE + 2 * PAD, PAD), PAD)
        peaks, kept = [None] * nq, {}
        k_buf[...] = qkv[hk, :].T

        def score(j, c):
            q, rr = slice(j * BT, (j + 1) * BT), slice(c * KC, (c + 1) * KC)
            s = mm(k_buf[rr, :], qkv[hq, q]) + bias[rr, q]
            kept[j, c] = s
            m = jnp.max(s.reshape(KC // 8, 8, BT), 0)
            peaks[j] = m if c == 0 else jnp.maximum(peaks[j], m)

        def expo(j, c):
            q, rr = slice(j * BT, (j + 1) * BT), slice(c * KC, (c + 1) * KC)
            if c == 0:
                peaks[j] = jnp.max(peaks[j], 0, keepdims=True)
            probs[h, rr, q] = jnp.exp2(kept.pop((j, c)) - peaks[j]).astype(BF)

        for j in range(nq + 1):
            for c in range(T // KC):
                if j < nq:
                    score(j, c)
                if j > 0:
                    expo(j - 1, c)
        o = mm(qkv[hv, :], probs[h])
        i = 1.0 / o[HEAD_DIM : HEAD_DIM + 1, :]
        inv[h] = i
        o = o * i
        ctx32[h] = o
        ctx[pl.ds(pl.multiple_of(h * PAD, PAD), PAD), :] = o.astype(BF)

        @pl.when(h == 1)
        def _():
            only(1, (1, 2, 3), lambda i: fetch(i).start())

        @pl.when(h == hs // 2)
        def _():
            only(0, (0,), pass_on)

        @pl.when(h == hs - 1)
        def _():
            only(0, (0,), lambda i: hand_on(i).wait_send())
            only(1, (0,), lambda i: hand_on(i).wait_recv())
            bias_sends[1].wait()
            head_weights(1)
            project(1)

        @pl.when(h == heads - 2)
        def _():
            only(1, (1, 2, 3), pass_on)

        return carry

    lax.fori_loop(0, heads, forward_head, 0)

    for k in ("comb", "up", "down", "thr", "corr", "gain", "shift", "cot"):
        loads[k].wait()
    only(1, (1, 2, 3), lambda i: hand_on(i).wait_send())
    only(0, (1, 2, 3), lambda i: hand_on(i).wait_recv())
    bias_sends[0].wait()

    def columns(x):
        k = x.shape[1]
        return jnp.broadcast_to(jnp.pad(x.astype(F32), ((0, 0), (0, up_to(k, 128) - k))), (128, up_to(k, 128))).T

    for s in range(2):
        cp[s * width : (s + 1) * width, :] = mm(sel, raw_comb[s]).astype(BF)
        upt[s * hst : s * hst + hid, :] = raw_up[s].T
        downn[s * hst : s * hst + hid, :] = raw_down[s].T
        upt[s * hst + hid : (s + 1) * hst, :] = jnp.zeros((hst - hid, D), BF)
        downn[s * hst + hid : (s + 1) * hst, :] = jnp.zeros((hst - hid, D), BF)
        thr_buf[s * hst : (s + 1) * hst, :] = columns(raw_thr[s])[0:hst, :]
    cpt[...] = cp[...].T
    for i in range(6):
        x = (raw_corr, raw_gain, raw_shift)[i // 2][...].astype(F32)
        vbuf[i * D : (i + 1) * D, :] = columns(x[i % 2 : i % 2 + 1, :])[0:D, :]
    one_row = jnp.where(lax.broadcasted_iota(jnp.int32, (8, T), 0) == 0, 1.0, 0.0).astype(BF)
    first_low[D : D + 8, :] = one_row
    acc[...] = jnp.zeros_like(acc)

    def vec(i):
        return wide(vbuf[i * D : (i + 1) * D, :])

    def norm(x):
        x = x - jnp.mean(x, 0, keepdims=True)
        rs = lax.rsqrt(jnp.mean(x * x, 0, keepdims=True) + EPS)
        return x * rs, rs

    def norm_back(dy, xhat, rs, g):
        d = dy * g
        return rs * (d - jnp.mean(d, 0, keepdims=True) - xhat * jnp.mean(d * xhat, 0, keepdims=True))

    lanes = lax.broadcasted_iota(jnp.int32, (D, 128), 1)

    def tally(i, v):
        acc[...] += jnp.where(lanes == i, jnp.sum(v, 1, keepdims=True), 0.0)

    HC = hst // 2

    def send_out(b):
        t = pl.ds(pl.multiple_of(b * BT, BT), BT)
        there = pl.ds(pl.multiple_of(me * T + b * BT, BT), BT)
        return remote(cot.at[:, t], lo_out.at[:, there], osend.at[b], orecv.at[b], peer)

    def middle(b, carry):
        t = pl.ds(pl.multiple_of(b * BT, BT), BT)
        att = mm(cpt[...], ctx[:, t])
        x1, rs1 = norm(tok[:, t].astype(F32) + att + vec(0))
        first = x1 * vec(2) + vec(4)
        low = first.astype(BF)
        first_low[0:D, t] = low
        for j in range(4):
            u = slice(j * HC, (j + 1) * HC)
            pre = mm(upt[u, :], low) + wide(thr_buf[u, :])
            cdf, pdf = phi_pair(pre)
            act[u, t] = (pre * cdf).astype(BF)
            dpre[u, t] = (cdf + pre * pdf).astype(BF)
        dn = mm(raw_down[0], act[0:hid, t]) + mm(raw_down[1], act[hst : hst + hid, t])
        x2, rs2 = norm(first + dn + vec(1))
        dy = cot[:, t].astype(F32)
        cot[:, t] = (x2 * vec(3) + vec(5)).astype(BF)
        send_out(b).start()
        tally(0, dy * x2)
        tally(1, dy)
        dr2 = norm_back(dy, x2, rs2, vec(3))
        tally(2, dr2)
        dd = dr2.astype(BF)
        d_down[:, t] = dd
        for j in range(4):
            u = slice(j * HC, (j + 1) * HC)
            dpre[u, t] = (mm(downn[u, :], dd) * dpre[u, t].astype(F32)).astype(BF)
        df = dr2 + mm(raw_up[0], dpre[0:hid, t]) + mm(raw_up[1], dpre[hst : hst + hid, t])
        tally(3, df * x1)
        tally(4, df)
        dr1 = norm_back(df, x1, rs1, vec(2))
        tally(5, dr1)
        bias[0:D, t] = dr1
        da = dr1.astype(BF)
        d_att[:, t] = da
        dctx[:, t] = mm(cp[...], da).astype(BF)
        return carry

    lax.fori_loop(0, T // BT, middle, 0)

    def all_of(ref, sem):
        pltpu.make_async_copy(ref, ref, sem).wait()

    def step(g, k):
        buf, half, quarter, gat = r[f"buf{g}"], r[f"half{g}"], r[f"quarter{g}"], r[f"gat{g}"]
        sizes, swap = plan.levels[g]
        rows_at = plan.blocks(g)
        top = len(sizes)
        strides = [1]
        for z in sizes:
            strides.append(strides[-1] * z)
        digit = [lax.rem(lax.div(chip, strides[j]), sizes[j]) for j in range(top)]
        spread = top - 1 if swap else top

        def member(j, i):
            d = lax.rem(digit[j] + i, sizes[j])
            return {"dp": (chip + (d - digit[j]) * strides[j]) * 2 + core}, d

        def held(j):
            return buf.at[core, 0] if j == 0 else r[f"sum{g}_{j - 1}"]

        def place(j):
            o = 0
            for i in range(j + 1):
                o = o + digit[i] * rows_at[i + 1]
            return pl.ds(pl.multiple_of(o, 16), rows_at[j + 1])

        def land(j):
            return r[f"land{g}_{j}"]

        def total(j):
            m = rows_at[j + 1]
            if j < spread:
                t = held(j)[pl.ds(pl.multiple_of(digit[j] * m, 16), m), :].astype(F32)
            else:
                t = held(j)[...].astype(F32)
            for i in range(sizes[j] - 1):
                t = t + land(j)[i].astype(F32)
            r[f"sum{g}_{j}"][...] = t.astype(BF)

        c1 = lambda: remote(buf.at[1 - core], half, gsend.at[g, 0], grecv.at[g, 0], sib)
        c2 = lambda: remote(buf.at[core, 1], quarter, gsend.at[g, 1], grecv.at[g, 1], peer)
        cl = lambda: remote(gat.at[core], gat.at[core], gsend.at[g, 2], grecv.at[g, 2], sib)
        own = lambda: pltpu.make_async_copy(r[f"sum{g}_{top - 1}"], gat.at[core, place(spread - 1), :], gloc.at[g])
        down_sem, up_sem = 3, 3 + top

        if k == 2:
            c1().wait()
            buf[core] = (buf[core].astype(F32) + half[...].astype(F32)).astype(BF)
        if k == 3:
            c2().wait()
            buf[core, 0] = (buf[core, 0].astype(F32) + quarter[...].astype(F32)).astype(BF)
        if 4 <= k < 4 + top:
            j = k - 4
            all_of(land(j), gsend.at[g, down_sem + j])
            all_of(land(j), grecv.at[g, down_sem + j])
            total(j)
        up = k - 3 - top
        if 1 <= up <= spread:
            j = spread - up
            if up == 1:
                own().wait()
            for sem in (gsend, grecv):
                part = gat.at[core, 0 : (sizes[j] - 1) * rows_at[j + 1], :]
                pltpu.make_async_copy(part, part, sem.at[g, up_sem + j]).wait()
        if k == 4 + top + spread:
            cl().wait()
            result(g).start()

        if k == 1:
            c1().start()
        if k == 2:
            c2().start()
        if 3 <= k < 3 + top:
            j = k - 3
            m = rows_at[j + 1]
            for i in range(1, sizes[j]):
                dev, d = member(j, i)
                src = held(j).at[pl.ds(pl.multiple_of(d * m, 16), m), :] if j < spread else held(j)
                remote(src, land(j).at[i - 1], gsend.at[g, down_sem + j], grecv.at[g, down_sem + j], dev).start()
        if 0 <= up < spread:
            j = spread - 1 - up
            if up == 0:
                own().start()
            for i in range(1, sizes[j]):
                dev, _ = member(j, i)
                src = r[f"sum{g}_{top - 1}"] if up == 0 else gat.at[core, place(j), :]
                remote(src, gat.at[core, place(j), :], gsend.at[g, up_sem + j], grecv.at[g, up_sem + j], dev).start()
        if k == 3 + top + spread:
            cl().start()

    def result(g):
        return pltpu.make_async_copy(r[f"gat{g}"], r[f"gat_out{g}"], gloc.at[g])

    def steps(g):
        sizes, swap = plan.levels[g]
        return 4 + 2 * len(sizes) - (1 if swap else 0)

    def put(g, s, base, x):
        buf = r[f"buf{g}"]
        hr = x.shape[0] // 2
        x = x.astype(BF)
        for l in range(up_to(x.shape[1], 128) // 128):
            wl = min(128, x.shape[1] - l * 128)
            for c in range(2):
                a = base + l * hr
                y = x[c * hr : (c + 1) * hr, l * 128 : l * 128 + wl]
                if wl == 64:
                    buf[c, s, a : a + hr // 2, :] = jnp.concatenate([y[: hr // 2], y[hr // 2 :]], 1)
                else:
                    buf[c, s, a : a + hr, 0:wl] = y

    def clear(g, rows_used):
        buf = r[f"buf{g}"]
        if rows_used < buf.shape[2]:
            buf[:, :, rows_used:, :] = jnp.zeros((2, 2, buf.shape[2] - rows_used, 128), BF)

    (gd, bd), (gu, bu), (gc, bc), (gs, bs) = plan.down, plan.up, plan.comb, plan.small
    for s in range(2):
        u = slice(s * hst, (s + 1) * hst)
        x = mm(d_down[...], act[u, :], NT)
        put(gd, s, bd, jnp.concatenate([x, jnp.zeros((8, hst), F32)], 0))
    clear(gd, plan.used[gd])
    step(gd, 1)
    sums = acc[...].T[0:8, :]
    hi = sums.astype(BF).astype(F32)
    for s in range(2):
        u = slice(s * hst, (s + 1) * hst)
        put(gu, s, bu, mm(first_low[...], dpre[u, :], NT))
        x = mm(ctx[s * width : (s + 1) * width, :], d_att[...], NT)
        put(gc, s, bc, jnp.concatenate([x, jnp.zeros((width, 8), F32)], 1))
        for l in range(3):
            wl = min(128, D - l * 128)
            x = jnp.concatenate([hi, sums - hi], 0)[:, l * 128 : l * 128 + wl].astype(BF)
            for c in range(2):
                r[f"buf{gs}"][c, s, bs + l * 16 : bs + (l + 1) * 16, 0:wl] = x
    clear(gu, plan.used[gu])
    step(gu, 1)
    first_low[0:D, :] = tok[...]

    lo_here = pltpu.make_async_copy(cot, lo_out.at[:, mine], lsem.at[13])
    lo_here.start()

    def part_grads(i):
        first, g = sum(plan.parts[:i]), plan.first_part + i
        for s in range(2):
            a = s * srows + first * TRIPLE
            put(g, s, 0, mm(dxt[a : a + plan.parts[i] * TRIPLE, :], first_low[...], NT))
        clear(g, plan.used[g])

    last = len(plan.rows) - 1

    def backward_head(i, carry):
        h = lax.rem(i, 2) * hs + lax.div(i, 2)
        hq = pl.ds(pl.multiple_of(h * TRIPLE, PAD), PAD)
        hk = pl.ds(pl.multiple_of(h * TRIPLE + PAD, PAD), PAD)
        hv = pl.ds(pl.multiple_of(h * TRIPLE + 2 * PAD, PAD), PAD)
        rowi = lax.broadcasted_iota(jnp.int32, (PAD, T), 0)
        scaled = (dctx[pl.ds(pl.multiple_of(h * PAD, PAD), PAD), :].astype(F32) * inv[h]).astype(BF).astype(F32)
        nd = -jnp.sum(scaled * ctx32[h], 0, keepdims=True)
        nh = nd.astype(BF).astype(F32)
        da = jnp.where(rowi == HEAD_DIM, nh, jnp.where(rowi == HEAD_DIM + 1, nd - nh, scaled)).astype(BF)
        k_buf[...] = qkv[hv, :].T
        qt, kt = qkv[hq, :], qkv[hk, :]
        dq = jnp.zeros((PAD, T), F32)
        for j in range(T // BT):
            rr = slice(j * BT, (j + 1) * BT)
            pk = probs[h, rr, :]
            dxt[hv, rr] = mm(da, pk, NT).astype(BF)
            ds = (pk.astype(F32) * mm(k_buf[rr, :], da)).astype(BF)
            dxt[hk, rr] = (mm(qt, ds, NT) * (1.0 / LOG2E)).astype(BF)
            dq = dq + mm(kt[:, rr], ds)
        dxt[hq, :] = (dq * SCALE).astype(BF)

        for at, todo in plan.schedule.items():
            @pl.when(i == at)
            def _(todo=todo):
                for what in todo:
                    if what == "part0":
                        part_grads(0)
                    else:
                        step(*what)
        return carry

    lax.fori_loop(0, heads, backward_head, 0)

    part_grads(len(plan.parts) - 1)
    w_rows = up_to(D, 16)

    def turn_weights():
        for a in range(0, 2 * srows, T):
            b = min(T, 2 * srows - a)
            o = a // T * w_rows
            dpre[o : o + D, 0:b] = wt[a : a + b, :].T

    def input_block(b):
        t = slice(b * BT, (b + 1) * BT)
        x = bias[0:D, t]
        for a in range(0, 2 * srows, T):
            e = min(T, 2 * srows - a)
            o = a // T * w_rows
            x = x + mm(dpre[o : o + D, 0:e], dxt[a : a + e, t])
        bias[0:D, t] = x
        d_down[:, t] = x.astype(BF)

    def move(b):
        t = slice(b * BT, (b + 1) * BT)
        return remote(d_down.at[:, t], dxp_out.at[:, t], xsend.at[b], xrecv.at[b], peer)

    dx_here = pltpu.make_async_copy(bias.at[0:D, :], dxo_out, lsem.at[14])
    done, sent = 0, None
    for what in plan.after:
        if what == "w":
            turn_weights()
        elif what == "send":
            sent = 0
        elif isinstance(what, int):
            input_block(what)
            done += 1
            if done == T // BT:
                dx_here.start()
        else:
            step(*what)
        while sent is not None and sent < done:
            move(sent).start()
            sent += 1
    for g in range(last + 1):
        result(g).wait()
    lo_here.wait()
    for b in range(T // BT):
        send_out(b).wait()
    dx_here.wait()
    for b in range(T // BT):
        move(b).wait()


def final_kernel(hs, plan, lo_in, dxo_in, dxp_in, *refs):
    ng = len(plan.rows)
    gat_in = refs[:ng]
    lo, dx, proj, off, comb, exp, thr, con, corr, gains, shifts, xp, xc, half, peer_half, own_half, lo_buf, sems, *gats = refs[ng:]
    D, T = dxp_in.shape
    me = lax.axis_index("tensor")
    own = pl.ds(pl.multiple_of(me * T, T), T)
    other = pl.ds(pl.multiple_of((1 - me) * T, T), T)
    fetch = [pltpu.make_async_copy(dxp_in, peer_half, sems.at[3]), pltpu.make_async_copy(dxo_in, own_half, sems.at[4]), pltpu.make_async_copy(lo_in, lo_buf, sems.at[5])]
    fetch += [pltpu.make_async_copy(a, b, sems.at[6 + i]) for i, (a, b) in enumerate(zip(gat_in, gats))]
    for c in fetch:
        c.start()
    copies = [
        pltpu.make_async_copy(half, dx.at[:, other], sems.at[0]), pltpu.make_async_copy(own_half, dx.at[:, own], sems.at[1]), pltpu.make_async_copy(lo_buf, lo, sems.at[2]),
    ]
    fetch[0].wait()
    half[...] = peer_half[...].astype(F32)
    copies[0].start()
    for i in (1, 2):
        fetch[i].wait()
        copies[i].start()
    for c in fetch[3:]:
        c.wait()

    (gd, bd), (gu, bu), (gc, bc), (gs, bs) = plan.down, plan.up, plan.comb, plan.small
    hid = exp.shape[1]
    width = hs * PAD
    sel = selector(hs)
    for c in range(2):
        for l in range(5):
            wl = min(128, hid - l * 128)
            ls = slice(l * 128, l * 128 + wl)
            rows = min(160, D - c * 160)
            con[c * 160 : c * 160 + rows, ls] = gats[gd][c, bd + l * 160 : bd + l * 160 + rows, 0:wl].astype(F32)
            exp[c * 160 : c * 160 + rows, ls] = gats[gu][c, bu + l * 160 : bu + l * 160 + rows, 0:wl].astype(F32)
            if c == 1:
                x = gats[gu][c, bu + l * 160 + 144 : bu + l * 160 + 160, 0:wl].astype(F32)
                thr[0:1, ls] = x[D - 160 - 144 : D - 160 - 143, :]

    def unfold(g, c, base, hr, l):
        a = base + l * hr
        if l < 2:
            return gats[g][c, a : a + hr, :]
        x = gats[g][c, a : a + hr // 2, :]
        return jnp.concatenate([x[:, 0:64], x[:, 64:128]], 0)

    for c in range(2):
        hr = width // 2
        for l in range(3):
            x = unfold(gc, c, bc, hr, l)
            xc[c * hr : (c + 1) * hr, l * 128 : l * 128 + x.shape[1]] = x
    comb[...] = mm(sel, xc[:, 0:D], TN)
    for l in range(3):
        wl = min(128, D - l * 128)
        ls = slice(l * 128, l * 128 + wl)
        a = bs + l * 16
        x = gats[gs][0, a : a + 16, 0:wl].astype(F32)
        x = x[0:8, :] + x[8:16, :]
        gains[1:2, ls] = x[0:1, :]
        shifts[1:2, ls] = x[1:2, :]
        corr[1:2, ls] = x[2:3, :]
        gains[0:1, ls] = x[3:4, :]
        shifts[0:1, ls] = x[4:5, :]
        corr[0:1, ls] = x[5:6, :]
    first = 0
    for i, hp in enumerate(plan.parts):
        hr = hp * TRIPLE // 2
        for c in range(2):
            for l in range(3):
                x = unfold(plan.first_part + i, c, 0, hr, l)
                for u in range(hr // 16):
                    v = c * (hr // 16) + u
                    h, p, q = first + v // 6, v % 6 // 2, v % 2
                    a = h * PAD + q * 16
                    xp[p, a : a + 16, l * 128 : l * 128 + x.shape[1]] = x[u * 16 : (u + 1) * 16, :]
        first += hp
    for p in range(3):
        proj[p] = mm(sel, xp[p, :, 0:D], TN)
    for i, p in ((0, 0), (1, 2)):
        t = mm(xp[p, :, 256:320], sel, TN)
        off[i : i + 1, :] = t[D - 256 : D - 255, :]
    for c in copies:
        c.wait()


def shards(n, tokens, projection, offsets, combiner, expansion, thresholds, contraction, corrections, gains, shifts, table_rows, table_columns, table_lengths, cotangent):
    tables = table_lengths.shape[0]
    T, D = tokens.shape[0] // tables, tokens.shape[1]
    part, hid = projection.shape[2], thresholds.shape[0]
    hs = part // HEAD_DIM
    W = hs * PAD
    R = hs * TRIPLE
    hst = up_to(hid, 16)

    ins = (
        tokens.T, cotangent.T, projection.transpose(0, 2, 1), combiner, expansion, contraction.T, thresholds.reshape(1, hid), offsets, corrections, gains, shifts,
        table_rows.reshape(-1, 128), table_columns.reshape(-1, 128), table_lengths,
    )
    plan = Plan(n, hs)
    H = plan.rows
    G = len(H)
    outs = [((D, tables * T), BF), ((D, T), F32), ((D, T), BF)] + [((2, h, 128), BF) for h in H]
    out_names = ["lo_out", "dxo_out", "dxp_out"] + [f"gat_out{g}" for g in range(G)]
    V = pltpu.VMEM
    sem = pltpu.SemaphoreType.DMA
    scratch = {
        "tok": V((D, T), BF), "cot": V((D, T), BF), "first_low": V((D + 8, T), BF), "d_down": V((D, T), BF), "d_att": V((D, T), BF),
        "raw_proj": V((2, 3, part, D), BF), "raw_comb": V((2, part, D), BF), "raw_up": V((2, D, hid), BF), "raw_down": V((2, D, hid), BF), "raw_thr": V((2, 1, hid), BF), "raw_offs": V((2, 2, part), BF), "raw_corr": V((2, D), BF), "raw_gain": V((2, D), BF), "raw_shift": V((2, D), BF),
        "wt": V((2 * R, D), BF), "cp": V((2 * W, D), BF), "cpt": V((D, 2 * W), BF), "upt": V((2 * hst, D), BF), "downn": V((2 * hst, D), BF),
        "qkv": V((2 * R, T), BF), "bias": V((T, T), F32), "probs": V((2 * hs, T, T), BF), "ctx32": V((2 * hs, PAD, T), F32), "ctx": V((2 * W, T), BF),
        "inv": V((2 * hs, 1, T), F32), "dctx": V((2 * W, T), BF), "dxt": V((max(2 * R, 2 * hst), T), BF), "dpre": V((2 * hst, T), BF),
        "vbuf": V((6 * D, 128), F32), "thr_buf": V((2 * hst, 128), F32), "off_buf": V((2 * R, 128), F32), "acc": V((D, 128), F32), "k_buf": V((T, PAD), BF),
        "rows": V((T // 128, 128), jnp.int32), "cols": V((T // 128, 128), jnp.int32),
        "lsem": sem((15,)), "wsend": sem((6, 2)), "wrecv": sem((6,)), "gsend": sem((G, 9)), "grecv": sem((G, 9)), "gloc": sem((G,)),
        "osend": sem((T // BT,)), "orecv": sem((T // BT,)), "xsend": sem((T // BT,)), "xrecv": sem((T // BT,)),
    }
    for g, h in enumerate(H):
        scratch[f"buf{g}"] = V((2, 2, h, 128), BF)
        scratch[f"half{g}"] = V((2, h, 128), BF)
        scratch[f"gat{g}"] = V((2, h, 128), BF)
        scratch[f"quarter{g}"] = V((h, 128), BF)
        sizes, _ = plan.levels[g]
        for j, z in enumerate(sizes):
            scratch[f"land{g}_{j}"] = V((z - 1, plan.blocks(g)[j + 1], 128), BF)
            scratch[f"sum{g}_{j}"] = V((plan.blocks(g)[j + 1], 128), BF)
    anywhere = pl.BlockSpec(memory_space=pl.ANY)
    vmem = pl.BlockSpec(memory_space=pltpu.VMEM)
    lo, dxo, dxp, *gats = pl.pallas_call(
        functools.partial(main_kernel, n, hs, plan, list(INPUTS) + out_names + list(scratch)),
        out_shape=[jax.ShapeDtypeStruct(s, d) for s, d in outs],
        in_specs=[anywhere] * (len(ins) - 1) + [pl.BlockSpec(memory_space=pltpu.SMEM)],
        out_specs=[anywhere] * len(outs),
        scratch_shapes=list(scratch.values()),
        compiler_params=pltpu.CompilerParams(vmem_limit_bytes=63 * 2 ** 20, collective_id=0, has_side_effects=True),
    )(*ins)
    finals = [
        ((D, tables * T), BF), ((D, tables * T), F32), ((3, part, D), F32), ((2, part), F32), ((part, D), F32), ((D, hid), F32),
        ((1, hid), F32), ((D, hid), F32), ((2, D), F32), ((2, D), F32), ((2, D), F32),
    ]
    lo, dx, proj, off, comb, exp, thr, con, corr, gn, sh = pl.pallas_call(
        functools.partial(final_kernel, hs, plan),
        out_shape=[jax.ShapeDtypeStruct(s, d) for s, d in finals],
        in_specs=[pl.BlockSpec(memory_space=pltpu.HBM)] * (3 + G),
        out_specs=[anywhere, anywhere] + [vmem] * 9,
        scratch_shapes=[V((3, W, 384), BF), V((W, 384), BF), V((D, T), F32), V((D, T), BF), V((D, T), F32), V((D, tables * T), BF), sem((6 + G,))] + [V((2, h, 128), BF) for h in H],
        compiler_params=pltpu.CompilerParams(vmem_limit_bytes=62 * 2 ** 20),
    )(lo, dxo, dxp, *gats)
    return lo.T, dx.T, proj.transpose(0, 2, 1), off, comb, exp, thr.reshape(hid), con.T, corr, gn, sh


def solution(mesh):
    return jax.shard_map(
        functools.partial(shards, mesh.shape["dp"] // 2),
        mesh=mesh,
        in_specs=(
            P("dp", None), P(None, None, "tensor"), P(None, "tensor"), P("tensor", None), P(None, "tensor"), P("tensor"),
            P("tensor", None), P(), P(), P(), P("dp"), P("dp"), P("dp"), P("dp", None),
        ),
        out_specs=(
            P("dp", None), P("dp", None), P(None, None, "tensor"), P(None, "tensor"), P("tensor", None), P(None, "tensor"),
            P("tensor"), P("tensor", None), P(), P(), P(),
        ),
        check_vma=False,
    )
```

```python
import functools

import jax
import jax.numpy as jnp
from jax import lax
from jax.experimental import pallas as pl
from jax.experimental.pallas import tpu as pltpu
from jax.sharding import PartitionSpec as P

HEAD_DIM = 26
PAD = 32
TRIPLE = 3 * PAD
EPS = 1e-05
MASKED = -1e30
SCALE = HEAD_DIM ** -0.5
LOG2E = 1.4426950408889634
BF = jnp.bfloat16
F32 = jnp.float32
NN = (((1,), (0,)), ((), ()))
NT = (((1,), (1,)), ((), ()))
TN = (((0,), (0,)), ((), ()))
BT = 256
MESH = pl.DeviceIdType.MESH


def mm(a, b, dims=NN):
    return lax.dot_general(a, b, dims, preferred_element_type=F32)


def up_to(x, m):
    return -(-x // m) * m


def wide(x):
    return jnp.concatenate([x, x], 1)


def phi_pair(x):
    z = jnp.abs(x)
    t = 1.0 / (1.0 + (0.3275911 * 0.5 ** 0.5) * z)
    e = jnp.exp2(x * x * (-0.5 * LOG2E))
    poly = ((((0.5307027145 * t - 0.7265760135) * t + 0.7107068705) * t - 0.142248368) * t + 0.127414796) * t
    tail = poly * e
    return jnp.where(x < 0, tail, 1.0 - tail), e * 0.3989422804014327


def selector(hs):
    r = lax.broadcasted_iota(jnp.int32, (hs * PAD, hs * HEAD_DIM), 0)
    c = lax.broadcasted_iota(jnp.int32, (hs * PAD, hs * HEAD_DIM), 1)
    inside = (r & (PAD - 1)) < HEAD_DIM
    return jnp.where(inside & (c == r - (PAD - HEAD_DIM) * (r >> 5)), 1.0, 0.0).astype(BF)


INPUTS = (
    "tok_in", "cot_in", "proj_in", "comb_in", "up_in", "down_in", "thr_in", "offs_in", "corr_in", "gain_in", "shift_in", "rows_in", "cols_in", "len_in",
)


class Plan:
    def __init__(self, n, hs):
        feed, out = 5 * 160, 5 * (hs * PAD // 4)
        self.parts = PARTS
        self.down, self.up, self.comb, self.small = (0, 0), (1, 0), (1, feed), (1, feed + out)
        self.used = [feed, feed + out + 48] + [5 * (hp * TRIPLE // 4) for hp in self.parts]
        self.first_part = 2
        chain, left = [], n
        while left > 1:
            chain.append(min(4, left))
            left //= chain[-1]
        self.levels = [([n], False) if flat and n <= 8 else (chain, True) for flat in FLAT]
        self.rows = []
        for x, (sizes, swap) in zip(self.used, self.levels):
            cut = 1
            for z in sizes[:-1] if swap else sizes:
                cut *= z
            self.rows.append(up_to(x, 16 * cut))
        self.schedule = SCHEDULE
        self.after = AFTER

    def blocks(self, g):
        sizes, swap = self.levels[g]
        out = [self.rows[g]]
        for j, z in enumerate(sizes):
            out.append(out[-1] if swap and j == len(sizes) - 1 else out[-1] // z)
        return out


PARTS = (4, 2)
LAG, STAGES, EARLY = 1, 15, 2
FLAT = (False, False, False, True)
SCHEDULE = {0: [(1, 2)], 2: [(0, 3)], 3: ["lo", "part0", (2, 1), (0, 4), (1, 3)], 4: [(2, 2), (0, 5)], 5: [(0, 6), (1, 4)]}
AFTER = [(3, 1), 0, (3, 2), "send", 1, (2, 3), (0, 7), (1, 5), 2, 3, (3, 3), (2, 4), (1, 6), (3, 4), (2, 5), (1, 7), (2, 6), (3, 5), (2, 7), (3, 6)]


def main_kernel(n, hs, plan, names, *refs):
    r = dict(zip(names, refs))
    tok_in, cot_in, proj_in, comb_in, up_in, down_in, thr_in, offs_in, corr_in, gain_in, shift_in, rows_in, cols_in, len_in = (r[k] for k in INPUTS)
    lo_out, dxo_out, dxp_out = r["lo_out"], r["dxo_out"], r["dxp_out"]
    tok, cot, first_low, d_down, d_att = (r[k] for k in ("tok", "cot", "first_low", "d_down", "d_att"))
    raw_proj, raw_comb, raw_up, raw_down = (r[k] for k in ("raw_proj", "raw_comb", "raw_up", "raw_down"))
    raw_thr, raw_offs, raw_corr, raw_gain, raw_shift = (r[k] for k in ("raw_thr", "raw_offs", "raw_corr", "raw_gain", "raw_shift"))
    wt, cp, cpt, upt, downn = (r[k] for k in ("wt", "cp", "cpt", "upt", "downn"))
    qkv, bias, probs, ctx32, ctx, inv, dctx, dxt, dpre = (
        r[k] for k in ("qkv", "bias", "probs", "ctx32", "ctx", "inv", "dctx", "dxt", "dpre")
    )
    thr_buf, acc, k_buf, da_buf = (r[k] for k in ("thr_buf", "acc", "k_buf", "da_buf"))
    rows, cols, lsem, wsend, wrecv, gsend, grecv, gloc, osend, orecv, xsend, xrecv = (
        r[k] for k in ("rows", "cols", "lsem", "wsend", "wrecv", "gsend", "grecv", "gloc", "osend", "orecv", "xsend", "xrecv")
    )
    act = dxt
    D, T = tok.shape
    heads = 2 * hs
    part = hs * HEAD_DIM
    width = hs * PAD
    srows = hs * TRIPLE
    hid = up_in.shape[1]
    hst = upt.shape[0] // 2

    me, dp = lax.axis_index("tensor"), lax.axis_index("dp")
    core, chip = lax.rem(dp, 2), lax.div(dp, 2)
    peer = {"tensor": 1 - me}
    sib = {"dp": dp + 1 - 2 * core}

    def chip_at(k):
        return lax.rem(chip + k, n)

    def on_chip(k):
        return {"dp": chip_at(k) * 2 + core}

    def remote(src, dst, ssem, rsem, dev):
        return pltpu.make_async_remote_copy(src_ref=src, dst_ref=dst, send_sem=ssem, recv_sem=rsem, device_id=dev, device_id_type=MESH)

    mine = pl.ds(pl.multiple_of(me * T, T), T)
    mine8 = pl.ds(pl.multiple_of(me * (T // 128), T // 128), T // 128)
    loads = {}
    for i, (k, a, b) in enumerate((
        ("proj", proj_in, raw_proj.at[0]), ("offs", offs_in, raw_offs.at[0]), ("tok", tok_in.at[:, mine], tok), ("rows", rows_in.at[mine8, :], rows),
        ("cols", cols_in.at[mine8, :], cols), ("comb", comb_in, raw_comb.at[0]), ("up", up_in, raw_up.at[0]), ("down", down_in, raw_down.at[0]),
        ("thr", thr_in, raw_thr.at[0]), ("corr", corr_in, raw_corr), ("gain", gain_in, raw_gain), ("shift", shift_in, raw_shift), ("cot", cot_in.at[:, mine], cot),
    )):
        loads[k] = pltpu.make_async_copy(a, b, lsem.at[i])
        loads[k].start()

    barrier = pltpu.get_barrier_semaphore()
    pl.semaphore_signal(barrier, inc=1, device_id=peer, device_id_type=MESH)
    pl.semaphore_signal(barrier, inc=1, device_id=sib, device_id_type=MESH)
    for k in range(1, n):
        pl.semaphore_signal(barrier, inc=1, device_id=on_chip(k), device_id_type=MESH)

    sel = selector(hs)
    lane = lax.broadcasted_iota(jnp.int32, (PAD, 128), 1)
    sub = lax.broadcasted_iota(jnp.int32, (PAD, 128), 0)
    extra = jnp.where((sub == HEAD_DIM) | (sub == HEAD_DIM + 1), 1.0, 0.0)

    def head_weights(s):
        off = mm(sel, raw_offs[s], NT)
        for p in range(3):
            x = mm(sel, raw_proj[s, p]).astype(BF)
            for h in range(hs):
                a = s * srows + h * TRIPLE + p * PAD
                wt[a : a + PAD, :] = x[h * PAD : (h + 1) * PAD, :]
                if p != 1:
                    col = jnp.broadcast_to(off[h * PAD : (h + 1) * PAD, p // 2 : p // 2 + 1], (PAD, 128))
                    thr_buf[a : a + PAD, :] = col + extra if p == 2 else col

    def project(s):
        def block(b, carry):
            t = pl.ds(pl.multiple_of(b * BT, BT), BT)
            x = mm(wt[s * srows : (s + 1) * srows, :], tok[:, t])
            for h in range(hs):
                for p in range(3):
                    a = s * srows + h * TRIPLE + p * PAD
                    y = x[h * TRIPLE + p * PAD : h * TRIPLE + (p + 1) * PAD, :]
                    if p != 1:
                        y = y + wide(thr_buf[a : a + PAD, :])
                    if p == 0:
                        y = y * (SCALE * LOG2E)
                    qkv[a : a + PAD, t] = y.astype(BF)
            return carry

        lax.fori_loop(0, T // BT, block, 0)

    loads["proj"].wait()
    loads["offs"].wait()
    head_weights(0)
    loads["tok"].wait()
    project(0)

    pl.semaphore_wait(barrier, n + 1)
    fetched = ((proj_in, raw_proj, 0), (comb_in, raw_comb, 1), (up_in, raw_up, 1), (down_in, raw_down, 1))

    def fetch(i):
        a, b, _ = fetched[i]
        return remote(a, b.at[1], wsend.at[i, 0], wrecv.at[i], peer)

    def hand_on(i):
        b = fetched[i][1]
        return remote(b.at[1], b.at[1], wsend.at[i, 1], wrecv.at[i], sib)

    def only(c, todo, what):
        @pl.when(core == c)
        def _():
            for i in todo:
                what(i)

    def pass_on(i):
        fetch(i).wait()
        hand_on(i).start()

    bias_sends = [
        remote(thr_in, raw_thr.at[1], wsend.at[4, 0], wrecv.at[4], peer),
        remote(offs_in, raw_offs.at[1], wsend.at[5, 0], wrecv.at[5], peer),
    ]
    for cpy in bias_sends:
        cpy.start()
    only(0, (0,), lambda i: fetch(i).start())

    loads["rows"].wait()
    loads["cols"].wait()
    length = jnp.where(me == 0, len_in[0], len_in[1])
    for j in range(T // 128):
        q = slice(j * 128, (j + 1) * 128)
        live = lax.broadcasted_iota(jnp.int32, (128, 128), 0) + j * 128 < length
        thr_buf[q, :] = jnp.where(live, jnp.broadcast_to(rows[j : j + 1, :].astype(F32), (128, 128)).T, jnp.nan)
        dxt[q, 0:128] = jnp.broadcast_to(cols[j : j + 1, :].astype(F32), (128, 128)).T.astype(BF)

    def visible(j, carry):
        q = pl.ds(pl.multiple_of(j * 128, 128), 128)
        rq = rows[pl.ds(j, 1), :].astype(F32)
        cq = cols[pl.ds(j, 1), :].astype(F32)
        rk = thr_buf[0:T, :]
        gap = rk * (rk - rq) * rq * (dxt[0:T, 0:128].astype(F32) - cq)
        bias[:, q] = jnp.where(gap == 0.0, 0.0, MASKED)
        return carry

    lax.fori_loop(0, T // 128, visible, 0)

    nq, KC = T // BT, 128

    def weigh(h, j):
        q = slice(j * BT, (j + 1) * BT)
        o = mm(qkv[pl.ds(pl.multiple_of(h * TRIPLE + 2 * PAD, PAD), PAD), :], probs[h, :, q])
        i = 1.0 / o[HEAD_DIM : HEAD_DIM + 1, :]
        inv[h, :, q] = i
        o = o * i
        ctx32[h, :, q] = o
        ctx[pl.ds(pl.multiple_of(h * PAD, PAD), PAD), q] = o.astype(BF)

    def forward_pair(i, carry):
        before = lax.rem(2 * i + heads - 2, heads)
        for e in range(2):
            k_buf[e] = qkv[pl.ds(pl.multiple_of((2 * i + e) * TRIPLE + PAD, PAD), PAD), :].T
        last_block = None
        for u in range(2 * nq + 1):
            if u < 2 * nq:
                e, j = divmod(u, nq)
                q = slice(j * BT, (j + 1) * BT)
                hq = pl.ds(pl.multiple_of((2 * i + e) * TRIPLE, PAD), PAD)
                scores, peak = [], None
            if last_block is not None:
                ph, pq, ps, pm = last_block
                pm = jnp.max(pm, 0, keepdims=True)
            for c in range(T // KC):
                rr = slice(c * KC, (c + 1) * KC)
                if u < 2 * nq:
                    x = mm(k_buf[e, rr, :], qkv[hq, q]) + bias[rr, q]
                    scores.append(x)
                    m = jnp.max(x.reshape(KC // 8, 8, BT), 0)
                    peak = m if c == 0 else jnp.maximum(peak, m)
                if last_block is not None:
                    probs[ph, rr, pq] = jnp.exp2(ps[c] - pm).astype(BF)
            if u < 2 * nq:
                weigh(before + e, j)
                last_block = (2 * i + e, q, scores, peak)

        @pl.when(i == 0)
        def _():
            only(1, (1, 2, 3), lambda i: fetch(i).start())

        @pl.when(i == hs // 4)
        def _():
            only(0, (0,), pass_on)

        @pl.when(i == hs // 2 - 1)
        def _():
            only(0, (0,), lambda i: hand_on(i).wait_send())
            only(1, (0,), lambda i: hand_on(i).wait_recv())
            bias_sends[1].wait()
            head_weights(1)
            project(1)

        @pl.when(i == hs - 2)
        def _():
            only(1, (1, 2, 3), pass_on)

        return carry

    lax.fori_loop(0, hs, forward_pair, 0)
    for e in range(2):
        for j in range(nq):
            weigh(heads - 2 + e, j)

    for k in ("comb", "up", "down", "thr", "corr", "gain", "shift", "cot"):
        loads[k].wait()
    only(1, (1, 2, 3), lambda i: hand_on(i).wait_send())
    only(0, (1, 2, 3), lambda i: hand_on(i).wait_recv())
    bias_sends[0].wait()

    def columns(x):
        k = x.shape[1]
        return jnp.broadcast_to(jnp.pad(x.astype(F32), ((0, 0), (0, up_to(k, 128) - k))), (128, up_to(k, 128))).T

    for s in range(2):
        cp[s * width : (s + 1) * width, :] = mm(sel, raw_comb[s]).astype(BF)
        upt[s * hst : s * hst + hid, :] = raw_up[s].T
        downn[s * hst : s * hst + hid, :] = raw_down[s].T
        upt[s * hst + hid : (s + 1) * hst, :] = jnp.zeros((hst - hid, D), BF)
        downn[s * hst + hid : (s + 1) * hst, :] = jnp.zeros((hst - hid, D), BF)
        thr_buf[s * hst : (s + 1) * hst, :] = columns(raw_thr[s])[0:hst, :]
    cpt[...] = cp[...].T
    for i in range(6):
        x = (raw_corr, raw_gain, raw_shift)[i // 2][...].astype(F32)
        bias[up_to(D, 16) : up_to(D, 16) + D, i * 128 : (i + 1) * 128] = columns(x[i % 2 : i % 2 + 1, :])[0:D, :]
    one_row = jnp.where(lax.broadcasted_iota(jnp.int32, (8, T), 0) == 0, 1.0, 0.0).astype(BF)
    first_low[D : D + 8, :] = one_row
    acc[...] = jnp.zeros_like(acc)

    def vec(i):
        return wide(bias[up_to(D, 16) : up_to(D, 16) + D, i * 128 : (i + 1) * 128])

    def norm(x):
        x = x - jnp.mean(x, 0, keepdims=True)
        rs = lax.rsqrt(jnp.mean(x * x, 0, keepdims=True) + EPS)
        return x * rs, rs

    def norm_back(dy, xhat, rs, g):
        d = dy * g
        return rs * (d - jnp.mean(d, 0, keepdims=True) - xhat * jnp.mean(d * xhat, 0, keepdims=True))

    lanes = lax.broadcasted_iota(jnp.int32, (D, 128), 1)

    def tally(i, v):
        acc[...] += jnp.where(lanes == i, jnp.sum(v, 1, keepdims=True), 0.0)

    HC = hst // 2

    def send_out(b):
        t = slice(b * BT, (b + 1) * BT)
        there = pl.ds(pl.multiple_of(me * T + b * BT, BT), BT)
        return remote(cot.at[:, t], lo_out.at[:, there], osend.at[b], orecv.at[b], peer)

    def block_stages(b):
        t = slice(b * BT, (b + 1) * BT)
        att = mm(cpt[...], ctx[:, t])
        yield
        x1, rs1 = norm(tok[:, t].astype(F32) + att + vec(0))
        first = x1 * vec(2) + vec(4)
        low = first.astype(BF)
        first_low[0:D, t] = low
        yield
        for j in range(4):
            u = slice(j * HC, (j + 1) * HC)
            pre = mm(upt[u, :], low) + wide(thr_buf[u, :])
            cdf, pdf = phi_pair(pre)
            act[u, t] = (pre * cdf).astype(BF)
            dpre[u, t] = (cdf + pre * pdf).astype(BF)
            yield
        dn = mm(raw_down[0], act[0:hid, t]) + mm(raw_down[1], act[hst : hst + hid, t])
        yield
        x2, rs2 = norm(first + dn + vec(1))
        dy = cot[:, t].astype(F32)
        cot[:, t] = (x2 * vec(3) + vec(5)).astype(BF)
        tally(0, dy * x2)
        tally(1, dy)
        dr2 = norm_back(dy, x2, rs2, vec(3))
        tally(2, dr2)
        dd = dr2.astype(BF)
        d_down[:, t] = dd
        if b < EARLY:
            send_out(b).start()
        yield
        for j in range(4):
            u = slice(j * HC, (j + 1) * HC)
            dpre[u, t] = (mm(downn[u, :], dd) * dpre[u, t].astype(F32)).astype(BF)
            yield
        df = dr2 + mm(raw_up[0], dpre[0:hid, t]) + mm(raw_up[1], dpre[hst : hst + hid, t])
        yield
        tally(3, df * x1)
        tally(4, df)
        dr1 = norm_back(df, x1, rs1, vec(2))
        tally(5, dr1)
        bias[0:D, t] = dr1
        da = dr1.astype(BF)
        d_att[:, t] = da
        yield
        dctx[:, t] = mm(cp[...], da).astype(BF)
        yield

    blocks = T // BT
    runs = [block_stages(b) for b in range(blocks)]
    for k in range(STAGES + LAG * (blocks - 1)):
        for b in range(blocks):
            if 0 <= k - LAG * b < STAGES:
                next(runs[b])

    def all_of(ref, sem):
        pltpu.make_async_copy(ref, ref, sem).wait()

    def step(g, k):
        buf, half, quarter, gat = r[f"buf{g}"], r[f"half{g}"], r[f"quarter{g}"], r[f"gat{g}"]
        sizes, swap = plan.levels[g]
        rows_at = plan.blocks(g)
        top = len(sizes)
        strides = [1]
        for z in sizes:
            strides.append(strides[-1] * z)
        digit = [lax.rem(lax.div(chip, strides[j]), sizes[j]) for j in range(top)]
        spread = top - 1 if swap else top

        def member(j, i):
            d = lax.rem(digit[j] + i, sizes[j])
            return {"dp": (chip + (d - digit[j]) * strides[j]) * 2 + core}, d

        def held(j):
            return buf.at[core, 0] if j == 0 else r[f"sum{g}_{j - 1}"]

        def place(j):
            o = 0
            for i in range(j + 1):
                o = o + digit[i] * rows_at[i + 1]
            return pl.ds(pl.multiple_of(o, 16), rows_at[j + 1])

        def land(j):
            return r[f"land{g}_{j}"]

        def total(j):
            m = rows_at[j + 1]
            if j < spread:
                t = held(j)[pl.ds(pl.multiple_of(digit[j] * m, 16), m), :].astype(F32)
            else:
                t = held(j)[...].astype(F32)
            for i in range(sizes[j] - 1):
                t = t + land(j)[i].astype(F32)
            r[f"sum{g}_{j}"][...] = t.astype(BF)

        c1 = lambda: remote(buf.at[1 - core], half, gsend.at[g, 0], grecv.at[g, 0], sib)
        c2 = lambda: remote(buf.at[core, 1], quarter, gsend.at[g, 1], grecv.at[g, 1], peer)
        cl = lambda: remote(gat.at[core], gat.at[core], gsend.at[g, 2], grecv.at[g, 2], sib)
        own = lambda: pltpu.make_async_copy(r[f"sum{g}_{top - 1}"], gat.at[core, place(spread - 1), :], gloc.at[g])
        down_sem, up_sem = 3, 3 + top

        if k == 2:
            c1().wait()
            buf[core] = (buf[core].astype(F32) + half[...].astype(F32)).astype(BF)
        if k == 3:
            c2().wait()
            buf[core, 0] = (buf[core, 0].astype(F32) + quarter[...].astype(F32)).astype(BF)
        if 4 <= k < 4 + top:
            j = k - 4
            all_of(land(j), gsend.at[g, down_sem + j])
            all_of(land(j), grecv.at[g, down_sem + j])
            total(j)
        up = k - 3 - top
        if 1 <= up <= spread:
            j = spread - up
            if up == 1:
                own().wait()
            for sem in (gsend, grecv):
                part = gat.at[core, 0 : (sizes[j] - 1) * rows_at[j + 1], :]
                pltpu.make_async_copy(part, part, sem.at[g, up_sem + j]).wait()
        if k == 4 + top + spread:
            cl().wait()
            result(g).start()

        if k == 1:
            c1().start()
        if k == 2:
            c2().start()
        if 3 <= k < 3 + top:
            j = k - 3
            m = rows_at[j + 1]
            for i in range(1, sizes[j]):
                dev, d = member(j, i)
                src = held(j).at[pl.ds(pl.multiple_of(d * m, 16), m), :] if j < spread else held(j)
                remote(src, land(j).at[i - 1], gsend.at[g, down_sem + j], grecv.at[g, down_sem + j], dev).start()
        if 0 <= up < spread:
            j = spread - 1 - up
            if up == 0:
                own().start()
            for i in range(1, sizes[j]):
                dev, _ = member(j, i)
                src = r[f"sum{g}_{top - 1}"] if up == 0 else gat.at[core, place(j), :]
                remote(src, gat.at[core, place(j), :], gsend.at[g, up_sem + j], grecv.at[g, up_sem + j], dev).start()
        if k == 3 + top + spread:
            cl().start()

    def result(g):
        return pltpu.make_async_copy(r[f"gat{g}"], r[f"gat_out{g}"], gloc.at[g])

    def steps(g):
        sizes, swap = plan.levels[g]
        return 4 + 2 * len(sizes) - (1 if swap else 0)

    def put(g, s, base, x):
        buf = r[f"buf{g}"]
        hr = x.shape[0] // 2
        x = x.astype(BF)
        for l in range(up_to(x.shape[1], 128) // 128):
            wl = min(128, x.shape[1] - l * 128)
            for c in range(2):
                a = base + l * hr
                y = x[c * hr : (c + 1) * hr, l * 128 : l * 128 + wl]
                if wl == 64:
                    buf[c, s, a : a + hr // 2, :] = jnp.concatenate([y[: hr // 2], y[hr // 2 :]], 1)
                else:
                    buf[c, s, a : a + hr, 0:wl] = y

    def clear(g, rows_used):
        buf = r[f"buf{g}"]
        if rows_used < buf.shape[2]:
            buf[:, :, rows_used:, :] = jnp.zeros((2, 2, buf.shape[2] - rows_used, 128), BF)

    (gd, bd), (gu, bu), (gc, bc), (gs, bs) = plan.down, plan.up, plan.comb, plan.small
    for s in range(2):
        u = slice(s * hst, (s + 1) * hst)
        x = mm(d_down[...], act[u, :], NT)
        put(gd, s, bd, jnp.concatenate([x, jnp.zeros((8, hst), F32)], 0))
    clear(gd, plan.used[gd])
    step(gd, 1)
    sums = acc[...].T[0:8, :]
    hi = sums.astype(BF).astype(F32)
    for s in range(2):
        u = slice(s * hst, (s + 1) * hst)
        put(gu, s, bu, mm(first_low[...], dpre[u, :], NT))
        x = mm(ctx[s * width : (s + 1) * width, :], d_att[...], NT)
        put(gc, s, bc, jnp.concatenate([x, jnp.zeros((width, 8), F32)], 1))
        for l in range(3):
            wl = min(128, D - l * 128)
            x = jnp.concatenate([hi, sums - hi], 0)[:, l * 128 : l * 128 + wl].astype(BF)
            for c in range(2):
                r[f"buf{gs}"][c, s, bs + l * 16 : bs + (l + 1) * 16, 0:wl] = x
    clear(gu, plan.used[gu])
    step(gu, 1)
    step(gd, 2)
    first_low[0:D, :] = tok[...]

    lo_here = pltpu.make_async_copy(cot, lo_out.at[:, mine], lsem.at[13])
    lo_here.start()

    def part_grads(i):
        first, g = sum(plan.parts[:i]), plan.first_part + i
        for s in range(2):
            a = s * srows + first * TRIPLE
            put(g, s, 0, mm(dxt[a : a + plan.parts[i] * TRIPLE, :], first_low[...], NT))
        clear(g, plan.used[g])

    last = len(plan.rows) - 1

    w_rows = up_to(D, 16)
    w_end = -(-2 * srows // T) * w_rows
    turned_p = [upt.at[0:T, 0:BT], downn.at[0:T, 0:BT]]
    free = up_to(w_end, 16)

    def turned_s(u, x=None):
        out = []
        for z in range(2):
            ls = slice((2 * u + z) * BT, (2 * u + z + 1) * BT)
            if x is not None:
                dpre[free : free + T // 2, ls] = x[z * (T // 2) : (z + 1) * (T // 2), :]
            else:
                out.append(dpre[free : free + T // 2, ls])
        return out

    def backward_pair(i, carry):
        heads_of = [i, hs + i]
        at = [[pl.ds(pl.multiple_of(h * TRIPLE + p * PAD, PAD), PAD) for p in range(3)] for h in heads_of]
        for e, h in enumerate(heads_of):
            rowi = lax.broadcasted_iota(jnp.int32, (PAD, T), 0)
            scaled = (dctx[pl.ds(pl.multiple_of(h * PAD, PAD), PAD), :].astype(F32) * inv[h]).astype(BF).astype(F32)
            nd = -jnp.sum(scaled * ctx32[h], 0, keepdims=True)
            nh = nd.astype(BF).astype(F32)
            da_buf[e] = jnp.where(rowi == HEAD_DIM, nh, jnp.where(rowi == HEAD_DIM + 1, nd - nh, scaled)).astype(BF)
            k_buf[e] = qkv[at[e][2], :].T
        dq = [None, None]

        def score_grads(u):
            e, j = divmod(u, nq)
            rr = slice(j * BT, (j + 1) * BT)
            pk = probs[heads_of[e], rr, :]
            turned_p[u % 2][...] = pk.T
            ds = (pk.astype(F32) * mm(k_buf[e, rr, :], da_buf[e])).astype(BF)
            turned_s(u % 2, ds.T)
            return ds

        def products(u, ds):
            e, j = divmod(u, nq)
            hq, hk, hv = at[e]
            rr = slice(j * BT, (j + 1) * BT)
            dxt[hv, rr] = mm(da_buf[e], turned_p[u % 2][...]).astype(BF)
            x, y = turned_s(u % 2)
            dk = mm(qkv[hq, 0 : T // 2], x) + mm(qkv[hq, T // 2 : T], y)
            dxt[hk, rr] = (dk * (1.0 / LOG2E)).astype(BF)
            z = mm(qkv[hk, rr], ds)
            dq[e] = z if j == 0 else dq[e] + z
            if j == nq - 1:
                dxt[hq, :] = (dq[e] * SCALE).astype(BF)

        held_ds = None
        for u in range(2 * nq + 1):
            now = score_grads(u) if u < 2 * nq else None
            if held_ds is not None:
                products(u - 1, held_ds)
            held_ds = now

        for when, todo in plan.schedule.items():
            @pl.when(i == when)
            def _(todo=todo):
                for what in todo:
                    if what == "lo":
                        for b in range(EARLY, T // BT):
                            send_out(b).start()
                    elif what == "part0":
                        part_grads(0)
                    else:
                        step(*what)
        return carry

    for a in range(0, 2 * srows, T):
        b = min(T, 2 * srows - a)
        o = a // T * w_rows
        dpre[o : o + D, 0:b] = wt[a : a + b, :].T
    lax.fori_loop(0, hs, backward_pair, 0)

    part_grads(len(plan.parts) - 1)
    def input_block(b):
        t = slice(b * BT, (b + 1) * BT)
        x = bias[0:D, t]
        for a in range(0, 2 * srows, T):
            e = min(T, 2 * srows - a)
            o = a // T * w_rows
            x = x + mm(dpre[o : o + D, 0:e], dxt[a : a + e, t])
        bias[0:D, t] = x
        d_down[:, t] = x.astype(BF)

    def move(b):
        t = slice(b * BT, (b + 1) * BT)
        return remote(d_down.at[:, t], dxp_out.at[:, t], xsend.at[b], xrecv.at[b], peer)

    dx_here = pltpu.make_async_copy(bias.at[0:D, :], dxo_out, lsem.at[14])
    done, sent = 0, None
    for what in plan.after:
        if what == "send":
            sent = 0
        elif isinstance(what, int):
            input_block(what)
            done += 1
            if done == T // BT:
                dx_here.start()
        else:
            step(*what)
        while sent is not None and sent < done:
            move(sent).start()
            sent += 1
    for g in range(last + 1):
        result(g).wait()
    lo_here.wait()
    for b in range(T // BT):
        send_out(b).wait()
    dx_here.wait()
    for b in range(T // BT):
        move(b).wait()


def final_kernel(hs, plan, lo_in, dxo_in, dxp_in, *refs):
    ng = len(plan.rows)
    gat_in = refs[:ng]
    lo, dx, proj, off, comb, exp, thr, con, corr, gains, shifts, xp, xc, half, peer_half, own_half, lo_buf, sems, *gats = refs[ng:]
    D, T = dxp_in.shape
    me = lax.axis_index("tensor")
    own = pl.ds(pl.multiple_of(me * T, T), T)
    other = pl.ds(pl.multiple_of((1 - me) * T, T), T)
    fetch = [pltpu.make_async_copy(dxp_in, peer_half, sems.at[3]), pltpu.make_async_copy(dxo_in, own_half, sems.at[4]), pltpu.make_async_copy(lo_in, lo_buf, sems.at[5])]
    fetch += [pltpu.make_async_copy(a, b, sems.at[6 + i]) for i, (a, b) in enumerate(zip(gat_in, gats))]
    for c in fetch:
        c.start()
    copies = [
        pltpu.make_async_copy(half, dx.at[:, other], sems.at[0]), pltpu.make_async_copy(own_half, dx.at[:, own], sems.at[1]), pltpu.make_async_copy(lo_buf, lo, sems.at[2]),
    ]
    fetch[0].wait()
    half[...] = peer_half[...].astype(F32)
    copies[0].start()
    for i in (1, 2):
        fetch[i].wait()
        copies[i].start()
    for c in fetch[3:]:
        c.wait()

    (gd, bd), (gu, bu), (gc, bc), (gs, bs) = plan.down, plan.up, plan.comb, plan.small
    hid = exp.shape[1]
    width = hs * PAD
    sel = selector(hs)
    for c in range(2):
        for l in range(5):
            wl = min(128, hid - l * 128)
            ls = slice(l * 128, l * 128 + wl)
            rows = min(160, D - c * 160)
            con[c * 160 : c * 160 + rows, ls] = gats[gd][c, bd + l * 160 : bd + l * 160 + rows, 0:wl].astype(F32)
            exp[c * 160 : c * 160 + rows, ls] = gats[gu][c, bu + l * 160 : bu + l * 160 + rows, 0:wl].astype(F32)
            if c == 1:
                x = gats[gu][c, bu + l * 160 + 144 : bu + l * 160 + 160, 0:wl].astype(F32)
                thr[0:1, ls] = x[D - 160 - 144 : D - 160 - 143, :]

    def unfold(g, c, base, hr, l):
        a = base + l * hr
        if l < 2:
            return gats[g][c, a : a + hr, :]
        x = gats[g][c, a : a + hr // 2, :]
        return jnp.concatenate([x[:, 0:64], x[:, 64:128]], 0)

    for c in range(2):
        hr = width // 2
        for l in range(3):
            x = unfold(gc, c, bc, hr, l)
            xc[c * hr : (c + 1) * hr, l * 128 : l * 128 + x.shape[1]] = x
    comb[...] = mm(sel, xc[:, 0:D], TN)
    for l in range(3):
        wl = min(128, D - l * 128)
        ls = slice(l * 128, l * 128 + wl)
        a = bs + l * 16
        x = gats[gs][0, a : a + 16, 0:wl].astype(F32)
        x = x[0:8, :] + x[8:16, :]
        gains[1:2, ls] = x[0:1, :]
        shifts[1:2, ls] = x[1:2, :]
        corr[1:2, ls] = x[2:3, :]
        gains[0:1, ls] = x[3:4, :]
        shifts[0:1, ls] = x[4:5, :]
        corr[0:1, ls] = x[5:6, :]
    first = 0
    for i, hp in enumerate(plan.parts):
        hr = hp * TRIPLE // 2
        for c in range(2):
            for l in range(3):
                x = unfold(plan.first_part + i, c, 0, hr, l)
                for u in range(hr // 16):
                    v = c * (hr // 16) + u
                    h, p, q = first + v // 6, v % 6 // 2, v % 2
                    a = h * PAD + q * 16
                    xp[p, a : a + 16, l * 128 : l * 128 + x.shape[1]] = x[u * 16 : (u + 1) * 16, :]
        first += hp
    for p in range(3):
        proj[p] = mm(sel, xp[p, :, 0:D], TN)
    for i, p in ((0, 0), (1, 2)):
        t = mm(xp[p, :, 256:320], sel, TN)
        off[i : i + 1, :] = t[D - 256 : D - 255, :]
    for c in copies:
        c.wait()


def shards(n, tokens, projection, offsets, combiner, expansion, thresholds, contraction, corrections, gains, shifts, table_rows, table_columns, table_lengths, cotangent):
    tables = table_lengths.shape[0]
    T, D = tokens.shape[0] // tables, tokens.shape[1]
    part, hid = projection.shape[2], thresholds.shape[0]
    hs = part // HEAD_DIM
    W = hs * PAD
    R = hs * TRIPLE
    hst = up_to(hid, 16)

    ins = (
        tokens.T, cotangent.T, projection.transpose(0, 2, 1), combiner, expansion, contraction.T, thresholds.reshape(1, hid), offsets, corrections, gains, shifts,
        table_rows.reshape(-1, 128), table_columns.reshape(-1, 128), table_lengths,
    )
    plan = Plan(n, hs)
    H = plan.rows
    G = len(H)
    outs = [((D, tables * T), BF), ((D, T), F32), ((D, T), BF)] + [((2, h, 128), BF) for h in H]
    out_names = ["lo_out", "dxo_out", "dxp_out"] + [f"gat_out{g}" for g in range(G)]
    V = pltpu.VMEM
    sem = pltpu.SemaphoreType.DMA
    scratch = {
        "tok": V((D, T), BF), "cot": V((D, T), BF), "first_low": V((D + 8, T), BF), "d_down": V((D, T), BF), "d_att": V((D, T), BF),
        "raw_proj": V((2, 3, part, D), BF), "raw_comb": V((2, part, D), BF), "raw_up": V((2, D, hid), BF), "raw_down": V((2, D, hid), BF), "raw_thr": V((2, 1, hid), BF), "raw_offs": V((2, 2, part), BF), "raw_corr": V((2, D), BF), "raw_gain": V((2, D), BF), "raw_shift": V((2, D), BF),
        "wt": V((2 * R, D), BF), "cp": V((2 * W, D), BF), "cpt": V((D, 2 * W), BF), "upt": V((2 * hst, D), BF), "downn": V((2 * hst, D), BF),
        "qkv": V((2 * R, T), BF), "bias": V((T, T), F32), "probs": V((2 * hs, T, T), BF), "ctx32": V((2 * hs, PAD, T), F32), "ctx": V((2 * W, T), BF),
        "inv": V((2 * hs, 1, T), F32), "dctx": V((2 * W, T), BF), "dxt": V((max(2 * R, 2 * hst), T), BF), "dpre": V((2 * hst, T), BF),
        "thr_buf": V((max(2 * hst, 2 * R), 128), F32), "acc": V((D, 128), F32), "k_buf": V((2, T, PAD), BF), "da_buf": V((2, PAD, T), BF),
        "rows": V((T // 128, 128), jnp.int32), "cols": V((T // 128, 128), jnp.int32),
        "lsem": sem((15,)), "wsend": sem((6, 2)), "wrecv": sem((6,)), "gsend": sem((G, 9)), "grecv": sem((G, 9)), "gloc": sem((G,)),
        "osend": sem((T // BT,)), "orecv": sem((T // BT,)), "xsend": sem((T // BT,)), "xrecv": sem((T // BT,)),
    }
    for g, h in enumerate(H):
        scratch[f"buf{g}"] = V((2, 2, h, 128), BF)
        scratch[f"half{g}"] = V((2, h, 128), BF)
        scratch[f"gat{g}"] = V((2, h, 128), BF)
        scratch[f"quarter{g}"] = V((h, 128), BF)
        sizes, _ = plan.levels[g]
        for j, z in enumerate(sizes):
            scratch[f"land{g}_{j}"] = V((z - 1, plan.blocks(g)[j + 1], 128), BF)
            scratch[f"sum{g}_{j}"] = V((plan.blocks(g)[j + 1], 128), BF)
    anywhere = pl.BlockSpec(memory_space=pl.ANY)
    vmem = pl.BlockSpec(memory_space=pltpu.VMEM)
    lo, dxo, dxp, *gats = pl.pallas_call(
        functools.partial(main_kernel, n, hs, plan, list(INPUTS) + out_names + list(scratch)),
        out_shape=[jax.ShapeDtypeStruct(s, d) for s, d in outs],
        in_specs=[anywhere] * (len(ins) - 1) + [pl.BlockSpec(memory_space=pltpu.SMEM)],
        out_specs=[anywhere] * len(outs),
        scratch_shapes=list(scratch.values()),
        compiler_params=pltpu.CompilerParams(vmem_limit_bytes=63 * 2 ** 20, collective_id=0, has_side_effects=True),
    )(*ins)
    finals = [
        ((D, tables * T), BF), ((D, tables * T), F32), ((3, part, D), F32), ((2, part), F32), ((part, D), F32), ((D, hid), F32),
        ((1, hid), F32), ((D, hid), F32), ((2, D), F32), ((2, D), F32), ((2, D), F32),
    ]
    lo, dx, proj, off, comb, exp, thr, con, corr, gn, sh = pl.pallas_call(
        functools.partial(final_kernel, hs, plan),
        out_shape=[jax.ShapeDtypeStruct(s, d) for s, d in finals],
        in_specs=[pl.BlockSpec(memory_space=pltpu.HBM)] * (3 + G),
        out_specs=[anywhere, anywhere] + [vmem] * 9,
        scratch_shapes=[V((3, W, 384), BF), V((W, 384), BF), V((D, T), F32), V((D, T), BF), V((D, T), F32), V((D, tables * T), BF), sem((6 + G,))] + [V((2, h, 128), BF) for h in H],
        compiler_params=pltpu.CompilerParams(vmem_limit_bytes=62 * 2 ** 20),
    )(lo, dxo, dxp, *gats)
    return lo.T, dx.T, proj.transpose(0, 2, 1), off, comb, exp, thr.reshape(hid), con.T, corr, gn, sh


def solution(mesh):
    return jax.shard_map(
        functools.partial(shards, mesh.shape["dp"] // 2),
        mesh=mesh,
        in_specs=(
            P("dp", None), P(None, None, "tensor"), P(None, "tensor"), P("tensor", None), P(None, "tensor"), P("tensor"),
            P("tensor", None), P(), P(), P(), P("dp"), P("dp"), P("dp"), P("dp", None),
        ),
        out_specs=(
            P("dp", None), P("dp", None), P(None, None, "tensor"), P(None, "tensor"), P("tensor", None), P(None, "tensor"),
            P("tensor"), P("tensor", None), P(), P(), P(),
        ),
        check_vma=False,
    )
```

```python
import functools

import jax
import jax.numpy as jnp
from jax import lax
from jax.experimental import pallas as pl
from jax.experimental.pallas import tpu as pltpu
from jax.sharding import PartitionSpec as P

HEAD_DIM = 26
PAD = 32
TRIPLE = 3 * PAD
EPS = 1e-05
MASKED = -1e30
SCALE = HEAD_DIM ** -0.5
LOG2E = 1.4426950408889634
BF = jnp.bfloat16
F32 = jnp.float32
NN = (((1,), (0,)), ((), ()))
NT = (((1,), (1,)), ((), ()))
TN = (((0,), (0,)), ((), ()))
BT = 256
MESH = pl.DeviceIdType.MESH


def mm(a, b, dims=NN):
    return lax.dot_general(a, b, dims, preferred_element_type=F32)


def up_to(x, m):
    return -(-x // m) * m


def wide(x):
    return jnp.concatenate([x, x], 1)


def phi_pair(x):
    z = jnp.abs(x)
    t = 1.0 / (1.0 + (0.3275911 * 0.5 ** 0.5) * z)
    e = jnp.exp2(x * x * (-0.5 * LOG2E))
    poly = ((((0.5307027145 * t - 0.7265760135) * t + 0.7107068705) * t - 0.142248368) * t + 0.127414796) * t
    tail = poly * e
    return jnp.where(x < 0, tail, 1.0 - tail), e * 0.3989422804014327


def selector(hs):
    r = lax.broadcasted_iota(jnp.int32, (hs * PAD, hs * HEAD_DIM), 0)
    c = lax.broadcasted_iota(jnp.int32, (hs * PAD, hs * HEAD_DIM), 1)
    inside = (r & (PAD - 1)) < HEAD_DIM
    return jnp.where(inside & (c == r - (PAD - HEAD_DIM) * (r >> 5)), 1.0, 0.0).astype(BF)


INPUTS = (
    "tok_in", "cot_in", "proj_in", "comb_in", "up_in", "down_in", "thr_in", "offs_in", "corr_in", "gain_in", "shift_in", "rows_in", "cols_in", "len_in",
)


class Plan:
    def __init__(self, n, hs):
        feed, out = 5 * 160, 5 * (hs * PAD // 4)
        self.parts = PARTS
        self.down, self.up, self.comb, self.small = (0, 0), (1, 0), (1, feed), (1, feed + out)
        self.used = [feed, feed + out + 48] + [5 * (hp * TRIPLE // 4) for hp in self.parts]
        self.first_part = 2
        chain, left = [], n
        while left > 1:
            chain.append(min(4, left))
            left //= chain[-1]
        self.levels = [([n], False) if flat and n <= 8 else (chain, True) for flat in FLAT]
        self.rows = []
        for x, (sizes, swap) in zip(self.used, self.levels):
            cut = 1
            for z in sizes[:-1] if swap else sizes:
                cut *= z
            self.rows.append(up_to(x, 16 * cut))
        self.schedule = SCHEDULE
        self.after = AFTER

    def blocks(self, g):
        sizes, swap = self.levels[g]
        out = [self.rows[g]]
        for j, z in enumerate(sizes):
            out.append(out[-1] if swap and j == len(sizes) - 1 else out[-1] // z)
        return out


PARTS = (4, 2)
LAG, STAGES, EARLY = 1, 15, 3
FLAT = (False, False, False, True)
SCHEDULE = {0: [(1, 2)], 2: [(0, 3)], 3: ["lo", "part0", (2, 1), (0, 4), (1, 3)], 4: [(2, 2), (0, 5)], 5: [(0, 6), (1, 4)]}
AFTER = [(3, 1), 0, (3, 2), "send", 1, (2, 3), (0, 7), (1, 5), 2, 3, (3, 3), (2, 4), (1, 6), (3, 4), (2, 5), (1, 7), (2, 6), (3, 5), (2, 7), (3, 6)]


def main_kernel(n, hs, plan, names, *refs):
    r = dict(zip(names, refs))
    tok_in, cot_in, proj_in, comb_in, up_in, down_in, thr_in, offs_in, corr_in, gain_in, shift_in, rows_in, cols_in, len_in = (r[k] for k in INPUTS)
    lo_out, dxo_out, dxp_out = r["lo_out"], r["dxo_out"], r["dxp_out"]
    tok, cot, first_low, d_down, d_att = (r[k] for k in ("tok", "cot", "first_low", "d_down", "d_att"))
    raw_proj, raw_comb, raw_up, raw_down = (r[k] for k in ("raw_proj", "raw_comb", "raw_up", "raw_down"))
    raw_thr, raw_offs, raw_corr, raw_gain, raw_shift = (r[k] for k in ("raw_thr", "raw_offs", "raw_corr", "raw_gain", "raw_shift"))
    wt, cp, cpt, upt, downn = (r[k] for k in ("wt", "cp", "cpt", "upt", "downn"))
    qkv, bias, probs, ctx32, ctx, inv, dctx, dxt, dpre = (
        r[k] for k in ("qkv", "bias", "probs", "ctx32", "ctx", "inv", "dctx", "dxt", "dpre")
    )
    thr_buf, acc, k_buf, da_buf = (r[k] for k in ("thr_buf", "acc", "k_buf", "da_buf"))
    rows, cols, lsem, wsend, wrecv, gsend, grecv, gloc, osend, orecv, xsend, xrecv = (
        r[k] for k in ("rows", "cols", "lsem", "wsend", "wrecv", "gsend", "grecv", "gloc", "osend", "orecv", "xsend", "xrecv")
    )
    act = dxt
    D, T = tok.shape
    heads = 2 * hs
    part = hs * HEAD_DIM
    width = hs * PAD
    srows = hs * TRIPLE
    hid = up_in.shape[1]
    hst = upt.shape[0] // 2

    me, dp = lax.axis_index("tensor"), lax.axis_index("dp")
    core, chip = lax.rem(dp, 2), lax.div(dp, 2)
    peer = {"tensor": 1 - me}
    sib = {"dp": dp + 1 - 2 * core}

    def chip_at(k):
        return lax.rem(chip + k, n)

    def on_chip(k):
        return {"dp": chip_at(k) * 2 + core}

    def remote(src, dst, ssem, rsem, dev):
        return pltpu.make_async_remote_copy(src_ref=src, dst_ref=dst, send_sem=ssem, recv_sem=rsem, device_id=dev, device_id_type=MESH)

    mine = pl.ds(pl.multiple_of(me * T, T), T)
    mine8 = pl.ds(pl.multiple_of(me * (T // 128), T // 128), T // 128)
    loads = {}
    for i, (k, a, b) in enumerate((
        ("proj", proj_in, raw_proj.at[0]), ("offs", offs_in, raw_offs.at[0]), ("tok", tok_in.at[:, mine], tok), ("rows", rows_in.at[mine8, :], rows),
        ("cols", cols_in.at[mine8, :], cols), ("comb", comb_in, raw_comb.at[0]), ("up", up_in, raw_up.at[0]), ("down", down_in, raw_down.at[0]),
        ("thr", thr_in, raw_thr.at[0]), ("corr", corr_in, raw_corr), ("gain", gain_in, raw_gain), ("shift", shift_in, raw_shift), ("cot", cot_in.at[:, mine], cot),
    )):
        loads[k] = pltpu.make_async_copy(a, b, lsem.at[i])
        loads[k].start()

    barrier = pltpu.get_barrier_semaphore()
    pl.semaphore_signal(barrier, inc=1, device_id=peer, device_id_type=MESH)
    pl.semaphore_signal(barrier, inc=1, device_id=sib, device_id_type=MESH)
    for k in range(1, n):
        pl.semaphore_signal(barrier, inc=1, device_id=on_chip(k), device_id_type=MESH)

    sel = selector(hs)
    lane = lax.broadcasted_iota(jnp.int32, (PAD, 128), 1)
    sub = lax.broadcasted_iota(jnp.int32, (PAD, 128), 0)
    extra = jnp.where((sub == HEAD_DIM) | (sub == HEAD_DIM + 1), 1.0, 0.0)

    def head_weights(s):
        off = mm(sel, raw_offs[s], NT)
        for p in range(3):
            x = mm(sel, raw_proj[s, p]).astype(BF)
            for h in range(hs):
                a = s * srows + h * TRIPLE + p * PAD
                wt[a : a + PAD, :] = x[h * PAD : (h + 1) * PAD, :]
                if p != 1:
                    col = jnp.broadcast_to(off[h * PAD : (h + 1) * PAD, p // 2 : p // 2 + 1], (PAD, 128))
                    thr_buf[a : a + PAD, :] = col + extra if p == 2 else col

    def project(s):
        def block(b, carry):
            t = pl.ds(pl.multiple_of(b * BT, BT), BT)
            x = mm(wt[s * srows : (s + 1) * srows, :], tok[:, t])
            for h in range(hs):
                for p in range(3):
                    a = s * srows + h * TRIPLE + p * PAD
                    y = x[h * TRIPLE + p * PAD : h * TRIPLE + (p + 1) * PAD, :]
                    if p != 1:
                        y = y + wide(thr_buf[a : a + PAD, :])
                    if p == 0:
                        y = y * (SCALE * LOG2E)
                    qkv[a : a + PAD, t] = y.astype(BF)
            return carry

        lax.fori_loop(0, T // BT, block, 0)

    loads["proj"].wait()
    loads["offs"].wait()
    head_weights(0)
    loads["tok"].wait()
    project(0)

    pl.semaphore_wait(barrier, n + 1)
    fetched = ((proj_in, raw_proj, 0), (comb_in, raw_comb, 1), (up_in, raw_up, 1), (down_in, raw_down, 1))

    def fetch(i):
        a, b, _ = fetched[i]
        return remote(a, b.at[1], wsend.at[i, 0], wrecv.at[i], peer)

    def hand_on(i):
        b = fetched[i][1]
        return remote(b.at[1], b.at[1], wsend.at[i, 1], wrecv.at[i], sib)

    def only(c, todo, what):
        @pl.when(core == c)
        def _():
            for i in todo:
                what(i)

    def pass_on(i):
        fetch(i).wait()
        hand_on(i).start()

    bias_sends = [
        remote(thr_in, raw_thr.at[1], wsend.at[4, 0], wrecv.at[4], peer),
        remote(offs_in, raw_offs.at[1], wsend.at[5, 0], wrecv.at[5], peer),
    ]
    for cpy in bias_sends:
        cpy.start()
    only(0, (0,), lambda i: fetch(i).start())

    loads["rows"].wait()
    loads["cols"].wait()
    length = jnp.where(me == 0, len_in[0], len_in[1])
    for j in range(T // 128):
        q = slice(j * 128, (j + 1) * 128)
        live = lax.broadcasted_iota(jnp.int32, (128, 128), 0) + j * 128 < length
        thr_buf[q, :] = jnp.where(live, jnp.broadcast_to(rows[j : j + 1, :].astype(F32), (128, 128)).T, jnp.nan)
        dxt[q, 0:128] = jnp.broadcast_to(cols[j : j + 1, :].astype(F32), (128, 128)).T.astype(BF)

    def visible(j, carry):
        q = pl.ds(pl.multiple_of(j * 128, 128), 128)
        rq = rows[pl.ds(j, 1), :].astype(F32)
        cq = cols[pl.ds(j, 1), :].astype(F32)
        rk = thr_buf[0:T, :]
        gap = rk * (rk - rq) * rq * (dxt[0:T, 0:128].astype(F32) - cq)
        bias[:, q] = jnp.where(gap == 0.0, 0.0, MASKED)
        return carry

    lax.fori_loop(0, T // 128, visible, 0)

    nq, KC = T // BT, 128

    def weigh(h, j):
        q = slice(j * BT, (j + 1) * BT)
        o = mm(qkv[pl.ds(pl.multiple_of(h * TRIPLE + 2 * PAD, PAD), PAD), :], probs[h, :, q])
        i = 1.0 / o[HEAD_DIM : HEAD_DIM + 1, :]
        inv[h, :, q] = i
        o = o * i
        ctx32[h, :, q] = o
        ctx[pl.ds(pl.multiple_of(h * PAD, PAD), PAD), q] = o.astype(BF)

    def forward_pair(i, carry):
        before = lax.rem(2 * i + heads - 2, heads)
        for e in range(2):
            k_buf[e] = qkv[pl.ds(pl.multiple_of((2 * i + e) * TRIPLE + PAD, PAD), PAD), :].T
        last_block = None
        for u in range(2 * nq + 1):
            if u < 2 * nq:
                e, j = divmod(u, nq)
                q = slice(j * BT, (j + 1) * BT)
                hq = pl.ds(pl.multiple_of((2 * i + e) * TRIPLE, PAD), PAD)
                scores, peak = [], None
            if last_block is not None:
                ph, pq, ps, pm = last_block
                pm = jnp.max(pm, 0, keepdims=True)
            for c in range(T // KC):
                rr = slice(c * KC, (c + 1) * KC)
                if u < 2 * nq:
                    x = mm(k_buf[e, rr, :], qkv[hq, q]) + bias[rr, q]
                    scores.append(x)
                    m = jnp.max(x.reshape(KC // 8, 8, BT), 0)
                    peak = m if c == 0 else jnp.maximum(peak, m)
                if last_block is not None:
                    probs[ph, rr, pq] = jnp.exp2(ps[c] - pm).astype(BF)
            if u < 2 * nq:
                weigh(before + e, j)
                last_block = (2 * i + e, q, scores, peak)

        @pl.when(i == 0)
        def _():
            only(1, (1, 2, 3), lambda i: fetch(i).start())

        @pl.when(i == hs // 4)
        def _():
            only(0, (0,), pass_on)

        @pl.when(i == hs // 2 - 1)
        def _():
            only(0, (0,), lambda i: hand_on(i).wait_send())
            only(1, (0,), lambda i: hand_on(i).wait_recv())
            bias_sends[1].wait()
            head_weights(1)
            project(1)

        @pl.when(i == hs - 2)
        def _():
            only(1, (1, 2, 3), pass_on)

        return carry

    lax.fori_loop(0, hs, forward_pair, 0)
    for e in range(2):
        for j in range(nq):
            weigh(heads - 2 + e, j)

    for k in ("comb", "up", "down", "thr", "corr", "gain", "shift", "cot"):
        loads[k].wait()
    only(1, (1, 2, 3), lambda i: hand_on(i).wait_send())
    only(0, (1, 2, 3), lambda i: hand_on(i).wait_recv())
    bias_sends[0].wait()

    def columns(x):
        k = x.shape[1]
        return jnp.broadcast_to(jnp.pad(x.astype(F32), ((0, 0), (0, up_to(k, 128) - k))), (128, up_to(k, 128))).T

    for s in range(2):
        cp[s * width : (s + 1) * width, :] = mm(sel, raw_comb[s]).astype(BF)
        upt[s * hst : s * hst + hid, :] = raw_up[s].T
        downn[s * hst : s * hst + hid, :] = raw_down[s].T
        upt[s * hst + hid : (s + 1) * hst, :] = jnp.zeros((hst - hid, D), BF)
        downn[s * hst + hid : (s + 1) * hst, :] = jnp.zeros((hst - hid, D), BF)
        thr_buf[s * hst : (s + 1) * hst, :] = columns(raw_thr[s])[0:hst, :]
    cpt[...] = cp[...].T
    for i in range(6):
        x = (raw_corr, raw_gain, raw_shift)[i // 2][...].astype(F32)
        bias[up_to(D, 16) : up_to(D, 16) + D, i * 128 : (i + 1) * 128] = columns(x[i % 2 : i % 2 + 1, :])[0:D, :]
    one_row = jnp.where(lax.broadcasted_iota(jnp.int32, (8, T), 0) == 0, 1.0, 0.0).astype(BF)
    first_low[D : D + 8, :] = one_row
    acc[...] = jnp.zeros_like(acc)

    def vec(i):
        return wide(bias[up_to(D, 16) : up_to(D, 16) + D, i * 128 : (i + 1) * 128])

    def norm(x):
        x = x - jnp.mean(x, 0, keepdims=True)
        rs = lax.rsqrt(jnp.mean(x * x, 0, keepdims=True) + EPS)
        return x * rs, rs

    def norm_back(dy, xhat, rs, g):
        d = dy * g
        return rs * (d - jnp.mean(d, 0, keepdims=True) - xhat * jnp.mean(d * xhat, 0, keepdims=True))

    lanes = lax.broadcasted_iota(jnp.int32, (D, 128), 1)

    def tally(i, v):
        acc[...] += jnp.where(lanes == i, jnp.sum(v, 1, keepdims=True), 0.0)

    HC = hst // 2

    def send_out(b):
        t = slice(b * BT, (b + 1) * BT)
        there = pl.ds(pl.multiple_of(me * T + b * BT, BT), BT)
        return remote(cot.at[:, t], lo_out.at[:, there], osend.at[b], orecv.at[b], peer)

    def block_stages(b):
        t = slice(b * BT, (b + 1) * BT)
        att = mm(cpt[...], ctx[:, t])
        yield
        x1, rs1 = norm(tok[:, t].astype(F32) + att + vec(0))
        first = x1 * vec(2) + vec(4)
        low = first.astype(BF)
        first_low[0:D, t] = low
        yield
        for j in range(4):
            u = slice(j * HC, (j + 1) * HC)
            pre = mm(upt[u, :], low) + wide(thr_buf[u, :])
            cdf, pdf = phi_pair(pre)
            act[u, t] = (pre * cdf).astype(BF)
            dpre[u, t] = (cdf + pre * pdf).astype(BF)
            yield
        dn = mm(raw_down[0], act[0:hid, t]) + mm(raw_down[1], act[hst : hst + hid, t])
        yield
        x2, rs2 = norm(first + dn + vec(1))
        dy = cot[:, t].astype(F32)
        cot[:, t] = (x2 * vec(3) + vec(5)).astype(BF)
        tally(0, dy * x2)
        tally(1, dy)
        dr2 = norm_back(dy, x2, rs2, vec(3))
        tally(2, dr2)
        dd = dr2.astype(BF)
        d_down[:, t] = dd
        if b < EARLY:
            send_out(b).start()
        yield
        for j in range(4):
            u = slice(j * HC, (j + 1) * HC)
            dpre[u, t] = (mm(downn[u, :], dd) * dpre[u, t].astype(F32)).astype(BF)
            yield
        df = dr2 + mm(raw_up[0], dpre[0:hid, t]) + mm(raw_up[1], dpre[hst : hst + hid, t])
        yield
        tally(3, df * x1)
        tally(4, df)
        dr1 = norm_back(df, x1, rs1, vec(2))
        tally(5, dr1)
        bias[0:D, t] = dr1
        da = dr1.astype(BF)
        d_att[:, t] = da
        yield
        dctx[:, t] = mm(cp[...], da).astype(BF)
        yield

    blocks = T // BT
    runs = [block_stages(b) for b in range(blocks)]
    for k in range(STAGES + LAG * (blocks - 1)):
        for b in range(blocks):
            if 0 <= k - LAG * b < STAGES:
                next(runs[b])

    def all_of(ref, sem):
        pltpu.make_async_copy(ref, ref, sem).wait()

    def step(g, k):
        buf, half, quarter, gat = r[f"buf{g}"], r[f"half{g}"], r[f"quarter{g}"], r[f"gat{g}"]
        sizes, swap = plan.levels[g]
        rows_at = plan.blocks(g)
        top = len(sizes)
        strides = [1]
        for z in sizes:
            strides.append(strides[-1] * z)
        digit = [lax.rem(lax.div(chip, strides[j]), sizes[j]) for j in range(top)]
        spread = top - 1 if swap else top

        def member(j, i):
            d = lax.rem(digit[j] + i, sizes[j])
            return {"dp": (chip + (d - digit[j]) * strides[j]) * 2 + core}, d

        def held(j):
            return buf.at[core, 0] if j == 0 else r[f"sum{g}_{j - 1}"]

        def place(j):
            o = 0
            for i in range(j + 1):
                o = o + digit[i] * rows_at[i + 1]
            return pl.ds(pl.multiple_of(o, 16), rows_at[j + 1])

        def land(j):
            return r[f"land{g}_{j}"]

        def total(j):
            m = rows_at[j + 1]
            if j < spread:
                t = held(j)[pl.ds(pl.multiple_of(digit[j] * m, 16), m), :].astype(F32)
            else:
                t = held(j)[...].astype(F32)
            for i in range(sizes[j] - 1):
                t = t + land(j)[i].astype(F32)
            r[f"sum{g}_{j}"][...] = t.astype(BF)

        c1 = lambda: remote(buf.at[1 - core], half, gsend.at[g, 0], grecv.at[g, 0], sib)
        c2 = lambda: remote(buf.at[core, 1], quarter, gsend.at[g, 1], grecv.at[g, 1], peer)
        cl = lambda: remote(gat.at[core], gat.at[core], gsend.at[g, 2], grecv.at[g, 2], sib)
        own = lambda: pltpu.make_async_copy(r[f"sum{g}_{top - 1}"], gat.at[core, place(spread - 1), :], gloc.at[g])
        down_sem, up_sem = 3, 3 + top

        if k == 2:
            c1().wait()
            buf[core] = (buf[core].astype(F32) + half[...].astype(F32)).astype(BF)
        if k == 3:
            c2().wait()
            buf[core, 0] = (buf[core, 0].astype(F32) + quarter[...].astype(F32)).astype(BF)
        if 4 <= k < 4 + top:
            j = k - 4
            all_of(land(j), gsend.at[g, down_sem + j])
            all_of(land(j), grecv.at[g, down_sem + j])
            total(j)
        up = k - 3 - top
        if 1 <= up <= spread:
            j = spread - up
            if up == 1:
                own().wait()
            for sem in (gsend, grecv):
                part = gat.at[core, 0 : (sizes[j] - 1) * rows_at[j + 1], :]
                pltpu.make_async_copy(part, part, sem.at[g, up_sem + j]).wait()
        if k == 4 + top + spread:
            cl().wait()
            result(g).start()

        if k == 1:
            c1().start()
        if k == 2:
            c2().start()
        if 3 <= k < 3 + top:
            j = k - 3
            m = rows_at[j + 1]
            for i in range(1, sizes[j]):
                dev, d = member(j, i)
                src = held(j).at[pl.ds(pl.multiple_of(d * m, 16), m), :] if j < spread else held(j)
                remote(src, land(j).at[i - 1], gsend.at[g, down_sem + j], grecv.at[g, down_sem + j], dev).start()
        if 0 <= up < spread:
            j = spread - 1 - up
            if up == 0:
                own().start()
            for i in range(1, sizes[j]):
                dev, _ = member(j, i)
                src = r[f"sum{g}_{top - 1}"] if up == 0 else gat.at[core, place(j), :]
                remote(src, gat.at[core, place(j), :], gsend.at[g, up_sem + j], grecv.at[g, up_sem + j], dev).start()
        if k == 3 + top + spread:
            cl().start()

    def result(g):
        return pltpu.make_async_copy(r[f"gat{g}"], r[f"gat_out{g}"], gloc.at[g])

    def steps(g):
        sizes, swap = plan.levels[g]
        return 4 + 2 * len(sizes) - (1 if swap else 0)

    def put(g, s, base, x):
        buf = r[f"buf{g}"]
        hr = x.shape[0] // 2
        x = x.astype(BF)
        for l in range(up_to(x.shape[1], 128) // 128):
            wl = min(128, x.shape[1] - l * 128)
            for c in range(2):
                a = base + l * hr
                y = x[c * hr : (c + 1) * hr, l * 128 : l * 128 + wl]
                if wl == 64:
                    buf[c, s, a : a + hr // 2, :] = jnp.concatenate([y[: hr // 2], y[hr // 2 :]], 1)
                else:
                    buf[c, s, a : a + hr, 0:wl] = y

    def clear(g, rows_used):
        buf = r[f"buf{g}"]
        if rows_used < buf.shape[2]:
            buf[:, :, rows_used:, :] = jnp.zeros((2, 2, buf.shape[2] - rows_used, 128), BF)

    (gd, bd), (gu, bu), (gc, bc), (gs, bs) = plan.down, plan.up, plan.comb, plan.small
    for s in range(2):
        u = slice(s * hst, (s + 1) * hst)
        x = mm(d_down[...], act[u, :], NT)
        put(gd, s, bd, jnp.concatenate([x, jnp.zeros((8, hst), F32)], 0))
    clear(gd, plan.used[gd])
    step(gd, 1)
    sums = acc[...].T[0:8, :]
    hi = sums.astype(BF).astype(F32)
    for s in range(2):
        u = slice(s * hst, (s + 1) * hst)
        put(gu, s, bu, mm(first_low[...], dpre[u, :], NT))
        x = mm(ctx[s * width : (s + 1) * width, :], d_att[...], NT)
        put(gc, s, bc, jnp.concatenate([x, jnp.zeros((width, 8), F32)], 1))
        for l in range(3):
            wl = min(128, D - l * 128)
            x = jnp.concatenate([hi, sums - hi], 0)[:, l * 128 : l * 128 + wl].astype(BF)
            for c in range(2):
                r[f"buf{gs}"][c, s, bs + l * 16 : bs + (l + 1) * 16, 0:wl] = x
    clear(gu, plan.used[gu])
    step(gu, 1)
    step(gd, 2)
    first_low[0:D, :] = tok[...]

    lo_here = pltpu.make_async_copy(cot, lo_out.at[:, mine], lsem.at[13])
    lo_here.start()

    def part_grads(i):
        first, g = sum(plan.parts[:i]), plan.first_part + i
        for s in range(2):
            a = s * srows + first * TRIPLE
            put(g, s, 0, mm(dxt[a : a + plan.parts[i] * TRIPLE, :], first_low[...], NT))
        clear(g, plan.used[g])

    last = len(plan.rows) - 1

    w_rows = up_to(D, 16)
    w_end = -(-2 * srows // T) * w_rows
    turned_p = [upt.at[0:T, 0:BT], downn.at[0:T, 0:BT]]
    free = up_to(w_end, 16)

    def turned_s(u, x=None):
        out = []
        for z in range(2):
            ls = slice((2 * u + z) * BT, (2 * u + z + 1) * BT)
            if x is not None:
                dpre[free : free + T // 2, ls] = x[z * (T // 2) : (z + 1) * (T // 2), :]
            else:
                out.append(dpre[free : free + T // 2, ls])
        return out

    def backward_pair(i, carry):
        heads_of = [i, hs + i]
        at = [[pl.ds(pl.multiple_of(h * TRIPLE + p * PAD, PAD), PAD) for p in range(3)] for h in heads_of]
        for e, h in enumerate(heads_of):
            rowi = lax.broadcasted_iota(jnp.int32, (PAD, T), 0)
            scaled = (dctx[pl.ds(pl.multiple_of(h * PAD, PAD), PAD), :].astype(F32) * inv[h]).astype(BF).astype(F32)
            nd = -jnp.sum(scaled * ctx32[h], 0, keepdims=True)
            nh = nd.astype(BF).astype(F32)
            da_buf[e] = jnp.where(rowi == HEAD_DIM, nh, jnp.where(rowi == HEAD_DIM + 1, nd - nh, scaled)).astype(BF)
            k_buf[e] = qkv[at[e][2], :].T
        dq = [None, None]

        def score_grads(u):
            e, j = divmod(u, nq)
            rr = slice(j * BT, (j + 1) * BT)
            pk = probs[heads_of[e], rr, :]
            turned_p[u % 2][...] = pk.T
            ds = (pk.astype(F32) * mm(k_buf[e, rr, :], da_buf[e])).astype(BF)
            turned_s(u % 2, ds.T)
            return ds

        def products(u, ds):
            e, j = divmod(u, nq)
            hq, hk, hv = at[e]
            rr = slice(j * BT, (j + 1) * BT)
            dxt[hv, rr] = mm(da_buf[e], turned_p[u % 2][...]).astype(BF)
            x, y = turned_s(u % 2)
            dk = mm(qkv[hq, 0 : T // 2], x) + mm(qkv[hq, T // 2 : T], y)
            dxt[hk, rr] = (dk * (1.0 / LOG2E)).astype(BF)
            z = mm(qkv[hk, rr], ds)
            dq[e] = z if j == 0 else dq[e] + z
            if j == nq - 1:
                dxt[hq, :] = (dq[e] * SCALE).astype(BF)

        held_ds = None
        for u in range(2 * nq + 1):
            now = score_grads(u) if u < 2 * nq else None
            if held_ds is not None:
                products(u - 1, held_ds)
            held_ds = now

        for when, todo in plan.schedule.items():
            @pl.when(i == when)
            def _(todo=todo):
                for what in todo:
                    if what == "lo":
                        for b in range(EARLY, T // BT):
                            send_out(b).start()
                    elif what == "part0":
                        part_grads(0)
                    else:
                        step(*what)
        return carry

    for a in range(0, 2 * srows, T):
        b = min(T, 2 * srows - a)
        o = a // T * w_rows
        dpre[o : o + D, 0:b] = wt[a : a + b, :].T
    lax.fori_loop(0, hs, backward_pair, 0)

    part_grads(len(plan.parts) - 1)
    def input_block(b):
        t = slice(b * BT, (b + 1) * BT)
        x = bias[0:D, t]
        for a in range(0, 2 * srows, T):
            e = min(T, 2 * srows - a)
            o = a // T * w_rows
            x = x + mm(dpre[o : o + D, 0:e], dxt[a : a + e, t])
        bias[0:D, t] = x
        d_down[:, t] = x.astype(BF)

    def move(b):
        t = slice(b * BT, (b + 1) * BT)
        return remote(d_down.at[:, t], dxp_out.at[:, t], xsend.at[b], xrecv.at[b], peer)

    dx_here = pltpu.make_async_copy(bias.at[0:D, :], dxo_out, lsem.at[14])
    done, sent = 0, None
    for what in plan.after:
        if what == "send":
            sent = 0
        elif isinstance(what, int):
            input_block(what)
            done += 1
            if done == T // BT:
                dx_here.start()
        else:
            step(*what)
        while sent is not None and sent < done:
            move(sent).start()
            sent += 1
    for g in range(last + 1):
        result(g).wait()
    lo_here.wait()
    for b in range(T // BT):
        send_out(b).wait()
    dx_here.wait()
    for b in range(T // BT):
        move(b).wait()


def final_kernel(hs, plan, lo_in, dxo_in, dxp_in, *refs):
    ng = len(plan.rows)
    gat_in = refs[:ng]
    lo, dx, proj, off, comb, exp, thr, con, corr, gains, shifts, xp, xc, half, peer_half, own_half, lo_buf, sems, *gats = refs[ng:]
    D, T = dxp_in.shape
    me = lax.axis_index("tensor")
    own = pl.ds(pl.multiple_of(me * T, T), T)
    other = pl.ds(pl.multiple_of((1 - me) * T, T), T)
    fetch = [pltpu.make_async_copy(dxp_in, peer_half, sems.at[3]), pltpu.make_async_copy(dxo_in, own_half, sems.at[4]), pltpu.make_async_copy(lo_in, lo_buf, sems.at[5])]
    fetch += [pltpu.make_async_copy(a, b, sems.at[6 + i]) for i, (a, b) in enumerate(zip(gat_in, gats))]
    for c in fetch:
        c.start()
    copies = [
        pltpu.make_async_copy(half, dx.at[:, other], sems.at[0]), pltpu.make_async_copy(own_half, dx.at[:, own], sems.at[1]), pltpu.make_async_copy(lo_buf, lo, sems.at[2]),
    ]
    fetch[0].wait()
    half[...] = peer_half[...].astype(F32)
    copies[0].start()
    for i in (1, 2):
        fetch[i].wait()
        copies[i].start()
    for c in fetch[3:]:
        c.wait()

    (gd, bd), (gu, bu), (gc, bc), (gs, bs) = plan.down, plan.up, plan.comb, plan.small
    hid = exp.shape[1]
    width = hs * PAD
    sel = selector(hs)
    for c in range(2):
        for l in range(5):
            wl = min(128, hid - l * 128)
            ls = slice(l * 128, l * 128 + wl)
            rows = min(160, D - c * 160)
            con[c * 160 : c * 160 + rows, ls] = gats[gd][c, bd + l * 160 : bd + l * 160 + rows, 0:wl].astype(F32)
            exp[c * 160 : c * 160 + rows, ls] = gats[gu][c, bu + l * 160 : bu + l * 160 + rows, 0:wl].astype(F32)
            if c == 1:
                x = gats[gu][c, bu + l * 160 + 144 : bu + l * 160 + 160, 0:wl].astype(F32)
                thr[0:1, ls] = x[D - 160 - 144 : D - 160 - 143, :]

    def unfold(g, c, base, hr, l):
        a = base + l * hr
        if l < 2:
            return gats[g][c, a : a + hr, :]
        x = gats[g][c, a : a + hr // 2, :]
        return jnp.concatenate([x[:, 0:64], x[:, 64:128]], 0)

    for c in range(2):
        hr = width // 2
        for l in range(3):
            x = unfold(gc, c, bc, hr, l)
            xc[c * hr : (c + 1) * hr, l * 128 : l * 128 + x.shape[1]] = x
    comb[...] = mm(sel, xc[:, 0:D], TN)
    for l in range(3):
        wl = min(128, D - l * 128)
        ls = slice(l * 128, l * 128 + wl)
        a = bs + l * 16
        x = gats[gs][0, a : a + 16, 0:wl].astype(F32)
        x = x[0:8, :] + x[8:16, :]
        gains[1:2, ls] = x[0:1, :]
        shifts[1:2, ls] = x[1:2, :]
        corr[1:2, ls] = x[2:3, :]
        gains[0:1, ls] = x[3:4, :]
        shifts[0:1, ls] = x[4:5, :]
        corr[0:1, ls] = x[5:6, :]
    first = 0
    for i, hp in enumerate(plan.parts):
        hr = hp * TRIPLE // 2
        for c in range(2):
            for l in range(3):
                x = unfold(plan.first_part + i, c, 0, hr, l)
                for u in range(hr // 16):
                    v = c * (hr // 16) + u
                    h, p, q = first + v // 6, v % 6 // 2, v % 2
                    a = h * PAD + q * 16
                    xp[p, a : a + 16, l * 128 : l * 128 + x.shape[1]] = x[u * 16 : (u + 1) * 16, :]
        first += hp
    for p in range(3):
        proj[p] = mm(sel, xp[p, :, 0:D], TN)
    for i, p in ((0, 0), (1, 2)):
        t = mm(xp[p, :, 256:320], sel, TN)
        off[i : i + 1, :] = t[D - 256 : D - 255, :]
    for c in copies:
        c.wait()


def shards(n, tokens, projection, offsets, combiner, expansion, thresholds, contraction, corrections, gains, shifts, table_rows, table_columns, table_lengths, cotangent):
    tables = table_lengths.shape[0]
    T, D = tokens.shape[0] // tables, tokens.shape[1]
    part, hid = projection.shape[2], thresholds.shape[0]
    hs = part // HEAD_DIM
    W = hs * PAD
    R = hs * TRIPLE
    hst = up_to(hid, 16)

    ins = (
        tokens.T, cotangent.T, projection.transpose(0, 2, 1), combiner, expansion, contraction.T, thresholds.reshape(1, hid), offsets, corrections, gains, shifts,
        table_rows.reshape(-1, 128), table_columns.reshape(-1, 128), table_lengths,
    )
    plan = Plan(n, hs)
    H = plan.rows
    G = len(H)
    outs = [((D, tables * T), BF), ((D, T), F32), ((D, T), BF)] + [((2, h, 128), BF) for h in H]
    out_names = ["lo_out", "dxo_out", "dxp_out"] + [f"gat_out{g}" for g in range(G)]
    V = pltpu.VMEM
    sem = pltpu.SemaphoreType.DMA
    scratch = {
        "tok": V((D, T), BF), "cot": V((D, T), BF), "first_low": V((D + 8, T), BF), "d_down": V((D, T), BF), "d_att": V((D, T), BF),
        "raw_proj": V((2, 3, part, D), BF), "raw_comb": V((2, part, D), BF), "raw_up": V((2, D, hid), BF), "raw_down": V((2, D, hid), BF), "raw_thr": V((2, 1, hid), BF), "raw_offs": V((2, 2, part), BF), "raw_corr": V((2, D), BF), "raw_gain": V((2, D), BF), "raw_shift": V((2, D), BF),
        "wt": V((2 * R, D), BF), "cp": V((2 * W, D), BF), "cpt": V((D, 2 * W), BF), "upt": V((2 * hst, D), BF), "downn": V((2 * hst, D), BF),
        "qkv": V((2 * R, T), BF), "bias": V((T, T), F32), "probs": V((2 * hs, T, T), BF), "ctx32": V((2 * hs, PAD, T), F32), "ctx": V((2 * W, T), BF),
        "inv": V((2 * hs, 1, T), F32), "dctx": V((2 * W, T), BF), "dxt": V((max(2 * R, 2 * hst), T), BF), "dpre": V((2 * hst, T), BF),
        "thr_buf": V((max(2 * hst, 2 * R), 128), F32), "acc": V((D, 128), F32), "k_buf": V((2, T, PAD), BF), "da_buf": V((2, PAD, T), BF),
        "rows": V((T // 128, 128), jnp.int32), "cols": V((T // 128, 128), jnp.int32),
        "lsem": sem((15,)), "wsend": sem((6, 2)), "wrecv": sem((6,)), "gsend": sem((G, 9)), "grecv": sem((G, 9)), "gloc": sem((G,)),
        "osend": sem((T // BT,)), "orecv": sem((T // BT,)), "xsend": sem((T // BT,)), "xrecv": sem((T // BT,)),
    }
    for g, h in enumerate(H):
        scratch[f"buf{g}"] = V((2, 2, h, 128), BF)
        scratch[f"half{g}"] = V((2, h, 128), BF)
        scratch[f"gat{g}"] = V((2, h, 128), BF)
        scratch[f"quarter{g}"] = V((h, 128), BF)
        sizes, _ = plan.levels[g]
        for j, z in enumerate(sizes):
            scratch[f"land{g}_{j}"] = V((z - 1, plan.blocks(g)[j + 1], 128), BF)
            scratch[f"sum{g}_{j}"] = V((plan.blocks(g)[j + 1], 128), BF)
    anywhere = pl.BlockSpec(memory_space=pl.ANY)
    vmem = pl.BlockSpec(memory_space=pltpu.VMEM)
    lo, dxo, dxp, *gats = pl.pallas_call(
        functools.partial(main_kernel, n, hs, plan, list(INPUTS) + out_names + list(scratch)),
        out_shape=[jax.ShapeDtypeStruct(s, d) for s, d in outs],
        in_specs=[anywhere] * (len(ins) - 1) + [pl.BlockSpec(memory_space=pltpu.SMEM)],
        out_specs=[anywhere] * len(outs),
        scratch_shapes=list(scratch.values()),
        compiler_params=pltpu.CompilerParams(vmem_limit_bytes=63 * 2 ** 20, collective_id=0, has_side_effects=True),
    )(*ins)
    finals = [
        ((D, tables * T), BF), ((D, tables * T), F32), ((3, part, D), F32), ((2, part), F32), ((part, D), F32), ((D, hid), F32),
        ((1, hid), F32), ((D, hid), F32), ((2, D), F32), ((2, D), F32), ((2, D), F32),
    ]
    lo, dx, proj, off, comb, exp, thr, con, corr, gn, sh = pl.pallas_call(
        functools.partial(final_kernel, hs, plan),
        out_shape=[jax.ShapeDtypeStruct(s, d) for s, d in finals],
        in_specs=[pl.BlockSpec(memory_space=pltpu.HBM)] * (3 + G),
        out_specs=[anywhere, anywhere] + [vmem] * 9,
        scratch_shapes=[V((3, W, 384), BF), V((W, 384), BF), V((D, T), F32), V((D, T), BF), V((D, T), F32), V((D, tables * T), BF), sem((6 + G,))] + [V((2, h, 128), BF) for h in H],
        compiler_params=pltpu.CompilerParams(vmem_limit_bytes=62 * 2 ** 20),
    )(lo, dxo, dxp, *gats)
    return lo.T, dx.T, proj.transpose(0, 2, 1), off, comb, exp, thr.reshape(hid), con.T, corr, gn, sh


def solution(mesh):
    return jax.shard_map(
        functools.partial(shards, mesh.shape["dp"] // 2),
        mesh=mesh,
        in_specs=(
            P("dp", None), P(None, None, "tensor"), P(None, "tensor"), P("tensor", None), P(None, "tensor"), P("tensor"),
            P("tensor", None), P(), P(), P(), P("dp"), P("dp"), P("dp"), P("dp", None),
        ),
        out_specs=(
            P("dp", None), P("dp", None), P(None, None, "tensor"), P(None, "tensor"), P("tensor", None), P(None, "tensor"),
            P("tensor"), P("tensor", None), P(), P(), P(),
        ),
        check_vma=False,
    )
```
